32 devices in a mesh: rows: 16 (over z, y, x), sub: 2 (over core).
Axes of the slice: x: 2, y: 2, z: 4, core: 2. Of those that a mesh axis runs over, the one named last changes fastest.
Arguments:
- affinity: bfloat16 [256, 3, 256, 256], P(('rows', 'sub')), may hold values from 0.0099487305 to 1
- old_basis: bfloat16 [65536, 64], P(('rows', 'sub')), may hold values from -1500 to 1500, as said below
- degrees: int32 [65536], P(('rows', 'sub')), may hold values from 10 to 90
- column_blocks: int32 [256, 3], P(('rows', 'sub')), may hold values from 0 to 255, as said below
- reorder: int32 [256, 256], P(('rows', 'sub')), may hold values from 0 to 255, each once within a row
Outputs:
- targets: float32 [65536, 64], P(('rows', 'sub'))
The draws below stay inside these ranges and needn't reach their ends.
Inputs may be any that keep to these rules, and one draw needn't show every extreme that they name: column_blocks[b, 0] = b; the other entries of row b are distinct, differ from b and lie within 2 of b; block row 0 names block 2. `old_basis`: entries of magnitude up to 1500.
All inputs are finite; a program needn't handle non-finite values.
Results may differ from the reference program's by a relative error of at most 0.0035.
Values may be sent and summed in bfloat16 or wider, within the bound.
No kernel may reach another device: no remote copies, remote signals or barrier semaphores. Data moves between devices by JAX's collectives and lax.ppermute only.
A program may use at most 64 MiB of HBM per device.

```python
import math
import jax
import jax.numpy as jnp
from jax import lax

BLK = 256
RANK = 64
NB = 3
REACH = 2
NBLK = 256
ITEMS = 65536


def draw_column_blocks(key, part):
    offsets = jnp.concatenate([jnp.arange(-REACH, 0, dtype=jnp.int32), jnp.arange(1, REACH + 1, dtype=jnp.int32)])
    spread = 2 * REACH
    row_ids = jnp.arange(NBLK, dtype=jnp.int32)[:, None]
    candidates = row_ids + offsets[None, :]
    invalid = ((candidates < 0) | (candidates >= NBLK)).astype(jnp.int32)
    scores = jax.random.randint(key, (NBLK, spread), 0, 1 << 20, dtype=jnp.int32) * spread
    scores = scores + jnp.arange(spread, dtype=jnp.int32)[None, :] + invalid * (1 << 28)
    order = jnp.argsort(scores, axis=1, stable=True)
    chosen = jnp.take_along_axis(candidates, order[:, :NB - 1], axis=1)
    return jnp.concatenate([row_ids, chosen], axis=1).astype(jnp.int32)


def draw_old_basis(key, part):
    first_key, second_key, third_key = jax.random.split(jax.random.fold_in(key, 7), 3)
    position = jnp.arange(ITEMS, dtype=jnp.float32)[:, None] / ITEMS
    row_scale = 10.0 ** jax.random.uniform(second_key, (ITEMS, 1), jnp.float32)
    column_scale = 10.0 ** jax.random.uniform(third_key, (1, RANK), jnp.float32)
    base = jnp.clip(jax.random.normal(first_key, (ITEMS, RANK), jnp.float32), -5.0, 5.0)
    trend = 1.7320508 ** position
    return (base * row_scale * column_scale * trend).astype(jnp.bfloat16)


def place_ends(values, own_key, least, largest):
    longest = values.shape.index(max(values.shape))
    spots = []
    for shift in (0, 1):
        where = [jax.random.randint(jax.random.fold_in(own_key, axis), (), 0, length) for axis, length in enumerate(values.shape)]
        where[longest] = (where[longest] + shift) % values.shape[longest]
        spots.append(tuple(where))
    return values.at[spots[0]].set(least).at[spots[1]].set(largest)


def block_levels(rng, extent, pieces, least, high):
    loudness = 1.0
    for dim, parts in pieces:
        draws = jax.random.uniform(jax.random.fold_in(jax.random.fold_in(rng, 6), dim), (parts,), jnp.float32, least / len(pieces), high / len(pieces))
        loudness = loudness * jnp.repeat(jnp.exp(draws), extent[dim] // parts).reshape((-1,) + (1,) * (len(extent) - 1 - dim))
    return loudness


def setup_inputs(seed: int = 0) -> dict:
    keys = jax.random.split(jax.random.key(seed), 6)
    affinity = jnp.clip(jnp.exp(math.log(1.0) - 4.61031033 * jax.random.uniform(keys[0], (NBLK, NB, BLK, BLK), jnp.float32) ** block_levels(keys[0], (NBLK, NB, BLK, BLK), ((0, 32),), -0.2, 0.2)), 0.0099487305, 1.0).astype(jnp.bfloat16)
    old_basis = draw_old_basis(jax.random.fold_in(keys[5], 71), 0)
    degrees = place_ends(jax.random.randint(keys[2], (ITEMS,), 10, 91), jax.random.fold_in(keys[2], 1), 10, 90).astype(jnp.int32)
    column_blocks = draw_column_blocks(jax.random.fold_in(keys[5], 71), 0)
    reorder = jax.vmap(lambda own: jax.random.permutation(own, BLK))(jax.random.split(keys[4], NBLK)).reshape((NBLK, BLK)).astype(jnp.int32)
    return dict(affinity=affinity, old_basis=old_basis, degrees=degrees, column_blocks=column_blocks, reorder=reorder)


def reference(affinity, old_basis, degrees, column_blocks, reorder):
    inverse_root = lax.rsqrt(degrees.astype(jnp.float32))[:, None]
    scaled = (inverse_root * old_basis.astype(jnp.float32)).astype(jnp.bfloat16)
    blocks = scaled.reshape(NBLK, BLK, RANK)

    def block_row(pair):
        aff_row, col_row = pair
        picked = blocks[col_row]
        total = jnp.zeros((BLK, RANK), jnp.float32)
        for slot in range(NB):
            total = total + jnp.dot(aff_row[slot].astype(jnp.float32), picked[slot].astype(jnp.float32), preferred_element_type=jnp.float32)
        return total
    product = lax.map(block_row, (affinity, column_blocks))
    image_rows = product.reshape(ITEMS, RANK) * inverse_root
    gram = jnp.dot(image_rows.T.astype(jnp.float32), image_rows.astype(jnp.float32), precision=lax.Precision.HIGHEST, preferred_element_type=jnp.float32)
    lower = jnp.linalg.cholesky(gram)
    solved = lax.linalg.triangular_solve(lower, image_rows.T, left_side=True, lower=True)
    clustered = (solved.T * jnp.sqrt(jnp.float32(ITEMS))).reshape(NBLK, BLK, RANK)
    targets = jnp.take_along_axis(clustered, reorder[:, :, None], axis=1)
    return targets.reshape(ITEMS, RANK)
```

```python
import functools
import math

import jax
import jax.numpy as jnp
from jax import lax
from jax.experimental import pallas as pl
from jax.experimental.pallas import tpu as pltpu
from jax.sharding import PartitionSpec as P

REACH = 2
AXES = ("rows", "sub")
LANES = 128
VMEM = pl.BlockSpec(memory_space=pltpu.VMEM)
SMEM = pl.BlockSpec(memory_space=pltpu.SMEM)


def rank_dot(a, b, contract):
    return lax.dot_general(a, b, ((contract[:1], contract[1:]), ((), ())), preferred_element_type=jnp.float32)


def scaled_piece(basis_ref, degrees_ref, piece):
    root = lax.rsqrt(degrees_ref[pl.ds(piece, 1), :].astype(jnp.float32))
    columns = pl.ds(pl.multiple_of(piece * LANES, LANES), LANES)
    return (root * basis_ref[:, columns].astype(jnp.float32)).astype(jnp.bfloat16)


def edges_kernel(width, place_ref, basis_ref, degrees_ref, near_ref, far_ref):
    pieces = width // LANES
    last = basis_ref.shape[1] // LANES - pieces
    odd = place_ref[0] % 2
    for i in range(pieces):
        near_ref[:, i * LANES:(i + 1) * LANES] = scaled_piece(basis_ref, degrees_ref, (1 - odd) * last + i)
        far_ref[:, i * LANES:(i + 1) * LANES] = scaled_piece(basis_ref, degrees_ref, odd * last + i)


def image_kernel(
    count, block, place_ref, columns_ref, basis_ref, degrees_ref, near_ref, far_ref, affinity_ref, image_ref, gram_ref, extended
):
    step = pl.program_id(0)
    per_block = block // LANES

    @pl.when(step == 0)
    def _():
        gram_ref[...] = jnp.zeros_like(gram_ref)
        for piece in range(count * per_block):
            b, c = divmod(piece, per_block)
            extended[REACH + b, :, c * LANES:(c + 1) * LANES] = scaled_piece(basis_ref, degrees_ref, piece)
        odd = place_ref[0] % 2
        near_at, far_at = (1 - odd) * (count + REACH), odd * (count + REACH)
        for b in range(REACH):
            extended[near_at + b] = near_ref[:, b * block:(b + 1) * block]
            extended[far_at + b] = far_ref[:, b * block:(b + 1) * block]

    first = place_ref[0] * count - REACH
    total = jnp.zeros((basis_ref.shape[0], block), jnp.float32)
    for slot in range(affinity_ref.shape[1]):
        picked = extended[columns_ref[step, slot] - first]
        total += rank_dot(picked, affinity_ref[0, slot], (1, 1))
    root = [
        lax.rsqrt(degrees_ref[pl.ds(step * per_block + c, 1), :].astype(jnp.float32)) for c in range(per_block)
    ]
    image = total * jnp.concatenate(root, axis=1)
    image_ref[...] = image
    gram_ref[...] += lax.dot_general(
        image, image, (((1,), (1,)), ((), ())), precision=lax.Precision.HIGHEST, preferred_element_type=jnp.float32
    )


def reorder_kernel(count, block, image_ref, reorder_ref, placed_ref):
    rank = image_ref.shape[0]
    source = lax.broadcasted_iota(jnp.int32, (block, block), 0)
    for b in range(count):
        columns = slice(b * block, (b + 1) * block)
        image = image_ref[:, columns]
        high = image.astype(jnp.bfloat16)
        low = (image - high.astype(jnp.float32)).astype(jnp.bfloat16)
        chosen = jnp.where(source == reorder_ref[b:b + 1, :], 1.0, 0.0).astype(jnp.bfloat16)
        moved = rank_dot(jnp.concatenate([high, low], axis=0), chosen, (1, 0))
        placed_ref[:, columns] = moved.astype(jnp.bfloat16)


def inverse_factor(gram):
    rank = gram.shape[0]
    rows = lax.broadcasted_iota(jnp.int32, (rank, rank), 0)
    columns = lax.broadcasted_iota(jnp.int32, (rank, rank), 1)
    state = jnp.concatenate([gram, jnp.where(rows == columns, 1.0, 0.0)], axis=1)
    below = lax.broadcasted_iota(jnp.int32, state.shape, 0)
    for k in range(rank):
        pivot = 1.0 / state[k:k + 1, k:k + 1]
        row = state[k:k + 1, :] * pivot
        state = jnp.where(below > k, state - state[:, k:k + 1] * row, state)
    diagonal = jnp.sum(jnp.where(rows == columns, state[:, :rank], 0.0), axis=1, keepdims=True)
    return lax.rsqrt(diagonal) * state[:, rank:]


def targets_kernel(total_items, gram_ref, placed_ref, targets_ref):
    rank = gram_ref.shape[0]
    inverse = inverse_factor(gram_ref[...]) * math.sqrt(total_items)
    high = inverse.astype(jnp.bfloat16)
    low = (inverse - high.astype(jnp.float32)).astype(jnp.bfloat16)
    left = jnp.concatenate([high, high, low], axis=1)
    right = jnp.concatenate([placed_ref[...], placed_ref[:rank, :]], axis=0)
    targets_ref[...] = rank_dot(left, right, (1, 0))


def body(mesh_size, affinity, old_basis, degrees, column_blocks, reorder):
    count, slots, block, _ = affinity.shape
    items, rank = old_basis.shape
    width = REACH * block
    basis = old_basis.T
    degree_rows = degrees.reshape(items // LANES, LANES)
    place = lax.axis_index(AXES).astype(jnp.int32).reshape(1)

    edge = jax.ShapeDtypeStruct((rank, width), jnp.bfloat16)
    near, far = pl.pallas_call(
        functools.partial(edges_kernel, width),
        out_shape=(edge, edge),
        in_specs=[SMEM, VMEM, VMEM],
        out_specs=(VMEM, VMEM),
    )(place, basis, degree_rows)
    near = lax.ppermute(near, AXES, [(i, i ^ 1) for i in range(mesh_size) if i ^ 1 < mesh_size])
    crossing = range(1, mesh_size - 1, 2)
    far = lax.ppermute(far, AXES, [(i, i + 1) for i in crossing] + [(i + 1, i) for i in crossing])

    whole = lambda shape: pl.BlockSpec(shape, lambda b: (0,) * len(shape))
    image, gram = pl.pallas_call(
        functools.partial(image_kernel, count, block),
        grid=(count,),
        out_shape=(jax.ShapeDtypeStruct((rank, items), jnp.float32), jax.ShapeDtypeStruct((rank, rank), jnp.float32)),
        in_specs=[
            SMEM,
            SMEM,
            whole((rank, items)),
            whole(degree_rows.shape),
            whole((rank, width)),
            whole((rank, width)),
            pl.BlockSpec((1, slots, block, block), lambda b: (b, 0, 0, 0)),
        ],
        out_specs=(pl.BlockSpec((rank, block), lambda b: (0, b)), whole((rank, rank))),
        scratch_shapes=[pltpu.VMEM((count + 2 * REACH, rank, block), jnp.bfloat16)],
    )(place, column_blocks, basis, degree_rows, near, far, affinity)

    if mesh_size & (mesh_size - 1):
        gram = lax.psum(gram, AXES)
    else:
        step = 1
        while step < mesh_size:
            mask = step | 1
            gram = gram + lax.ppermute(gram, AXES, [(i, i ^ mask) for i in range(mesh_size)])
            step *= 2

    placed = pl.pallas_call(
        functools.partial(reorder_kernel, count, block),
        out_shape=jax.ShapeDtypeStruct((2 * rank, items), jnp.bfloat16),
        in_specs=[VMEM, VMEM],
        out_specs=VMEM,
        cost_estimate=pl.CostEstimate(flops=4 * rank * items * block, bytes_accessed=8 * rank * items, transcendentals=0),
    )(image, reorder)

    targets = pl.pallas_call(
        functools.partial(targets_kernel, items * mesh_size),
        out_shape=jax.ShapeDtypeStruct((rank, items), jnp.float32),
        in_specs=[VMEM, VMEM],
        out_specs=VMEM,
    )(gram, placed)
    return targets.T


def solution(mesh):
    placed = (
        P(AXES, None, None, None),
        P(AXES, None),
        P(AXES),
        P(AXES, None),
        P(AXES, None),
    )
    mesh_size = mesh.shape["rows"] * mesh.shape["sub"]
    return jax.shard_map(
        functools.partial(body, mesh_size), mesh=mesh, in_specs=placed, out_specs=P(AXES, None), check_vma=False
    )
```

```python
import functools
import math

import jax
import jax.numpy as jnp
from jax import lax
from jax.experimental import pallas as pl
from jax.experimental.pallas import tpu as pltpu
from jax.sharding import PartitionSpec as P

REACH = 2
AXES = ("rows", "sub")
SUBLANES, LANES = 8, 128
VMEM = pl.BlockSpec(memory_space=pltpu.VMEM)
SMEM = pl.BlockSpec(memory_space=pltpu.SMEM)
HBM = pl.BlockSpec(memory_space=pltpu.HBM)
PARAMS = pltpu.CompilerParams(vmem_limit_bytes=16 << 20)


def in_vmem(x):
    return pltpu.with_memory_space_constraint(x, pltpu.VMEM)


def in_hbm(x):
    return pltpu.with_memory_space_constraint(x, pltpu.HBM)


def rank_dot(a, b, contract, precision=None):
    return lax.dot_general(
        a, b, ((contract[:1], contract[1:]), ((), ())), precision=precision, preferred_element_type=jnp.float32
    )


def gram_of(image):
    return rank_dot(image, image, (1, 1), lax.Precision.HIGHEST)


def inverse_root(degrees_ref, piece):
    return lax.rsqrt(degrees_ref[pl.ds(piece, 1), :].astype(jnp.float32))


def block_root(degrees_ref, b, block):
    pieces = block // LANES
    return jnp.concatenate([inverse_root(degrees_ref, b * pieces + c) for c in range(pieces)], axis=1)


def scaled(degrees_ref, piece, basis):
    return (inverse_root(degrees_ref, piece) * basis.astype(jnp.float32)).astype(jnp.bfloat16)


def edges_kernel(width, place_ref, basis_hbm, degrees_hbm, near_ref, far_ref, ends, degrees_ref, sems):
    items = basis_hbm.shape[1]
    pieces, last = width // LANES, (items - width) // LANES
    copies = [
        pltpu.make_async_copy(degrees_hbm, degrees_ref, sems.at[0]),
        pltpu.make_async_copy(basis_hbm.at[:, :width], ends.at[0], sems.at[1]),
        pltpu.make_async_copy(basis_hbm.at[:, items - width:], ends.at[1], sems.at[2]),
    ]
    for copy in copies:
        copy.start()
    odd = place_ref[0] % 2 == 1
    for copy in copies:
        copy.wait()
    for i in range(pieces):
        columns = slice(i * LANES, (i + 1) * LANES)
        head = scaled(degrees_ref, i, ends[0, :, columns])
        tail = scaled(degrees_ref, last + i, ends[1, :, columns])
        near_ref[:, columns] = jnp.where(odd, head, tail)
        far_ref[:, columns] = jnp.where(odd, tail, head)


def own_kernel(
    count, block, edges, place_ref, columns_hbm, basis_hbm, degrees_hbm, affinity_ref, partial_ref, gram_ref,
    columns_ref, degrees_ref, extended, basis_ref, sems
):
    pieces = block // LANES
    small = [
        pltpu.make_async_copy(columns_hbm, columns_ref, sems.at[0]),
        pltpu.make_async_copy(degrees_hbm, degrees_ref, sems.at[1]),
        pltpu.make_async_copy(basis_hbm, basis_ref, sems.at[2]),
    ]
    for copy in small:
        copy.start()
    for b in range(REACH):
        extended[b] = jnp.zeros_like(extended[b])
        extended[count + REACH + b] = jnp.zeros_like(extended[b])
    for copy in small:
        copy.wait()
    for piece in range(count * pieces):
        b, c = divmod(piece, pieces)
        extended[REACH + b, :, c * LANES:(c + 1) * LANES] = scaled(
            degrees_ref, piece, basis_ref[:, piece * LANES:(piece + 1) * LANES]
        )
    first = place_ref[0] * count - REACH
    inner = []
    for b in range(count):
        total = rank_dot(extended[REACH + b], affinity_ref[b, 0], (1, 1))
        for slot in range(1, affinity_ref.shape[1]):
            total += rank_dot(extended[columns_ref[slot, b] - first], affinity_ref[b, slot], (1, 1))
        if b not in edges:
            total *= block_root(degrees_ref, b, block)
            inner.append(total)
        partial_ref[:, b * block:(b + 1) * block] = total
    if inner:
        gram_ref[...] = gram_of(jnp.concatenate(inner, axis=1))
    else:
        gram_ref[...] = jnp.zeros_like(gram_ref)


def halo_kernel(
    count, block, edges, place_ref, columns_ref, degrees_ref, near_ref, far_ref, affinity_ref, partial_ref, inner_ref,
    image_ref, gram_ref, halo
):
    odd = place_ref[0] % 2
    for b in range(REACH):
        halo[(1 - odd) * REACH + b] = near_ref[:, b * block:(b + 1) * block]
        halo[odd * REACH + b] = far_ref[:, b * block:(b + 1) * block]
    halo[2 * REACH] = jnp.zeros_like(halo[0])
    first = place_ref[0] * count - REACH
    images = []
    for at, b in enumerate(edges):
        total = partial_ref[:, b * block:(b + 1) * block]
        for slot in range(1, affinity_ref.shape[1]):
            index = columns_ref[slot, b] - first
            index = jnp.where(index < REACH, index, jnp.where(index < REACH + count, 2 * REACH, index - count))
            total += rank_dot(halo[index], affinity_ref[b, slot], (1, 1))
        images.append(total * block_root(degrees_ref, b, block))
        image_ref[:, at * block:(at + 1) * block] = images[-1]
    gram_ref[...] = inner_ref[...] + gram_of(jnp.concatenate(images, axis=1))


def reorder_kernel(count, block, edges, inner_ref, outer_ref, reorder_ref, placed_ref):
    source = lax.broadcasted_iota(jnp.int32, (block, block), 0)
    for b in range(count):
        at = edges.index(b) if b in edges else b
        image = (outer_ref if b in edges else inner_ref)[:, at * block:(at + 1) * block]
        high = image.astype(jnp.bfloat16)
        low = (image - high.astype(jnp.float32)).astype(jnp.bfloat16)
        chosen = jnp.where(source == reorder_ref[b:b + 1, :], 1.0, 0.0).astype(jnp.bfloat16)
        moved = rank_dot(jnp.concatenate([high, low], axis=0), chosen, (1, 0))
        placed_ref[:, b * block:(b + 1) * block] = moved.astype(jnp.bfloat16)


def wide(x):
    return jnp.broadcast_to(x, (SUBLANES, LANES))


def inverse_factor(gram):
    rank = gram.shape[0]
    panels = rank // SUBLANES
    rows = lax.broadcasted_iota(jnp.int32, (rank, rank), 0)
    columns = lax.broadcasted_iota(jnp.int32, (rank, rank), 1)
    state = jnp.concatenate([gram, jnp.where(rows == columns, 1.0, 0.0)], axis=1)
    state = [state[SUBLANES * q:SUBLANES * (q + 1)] for q in range(panels)]
    sublane = lax.broadcasted_iota(jnp.int32, (SUBLANES, LANES), 0)
    span = range(SUBLANES)
    out = []
    for p in range(panels):
        spread = [[wide(state[q][:, SUBLANES * p + j:SUBLANES * p + j + 1]) for j in span] for q in range(p, panels)]
        pivot = [[wide(spread[0][j][i:i + 1, :]) for j in range(i + 1)] for i in span]
        old = [wide(state[p][i:i + 1, :]) for i in span]
        inverse, unit, new = [], [], []
        for i in span:
            inverse.append(1.0 / pivot[i][i])
            factor = [pivot[i][m] * inverse[m] for m in range(i)]
            line = []
            for m in range(i):
                entry = factor[m]
                for k in range(m + 1, i):
                    entry = entry + factor[k] * unit[k][m]
                line.append(-entry)
            unit.append(line)
            row = old[i]
            for m in range(i):
                row = row + line[m] * old[m]
            new.append(row)
            for k in range(i + 1, SUBLANES):
                weight = pivot[k][i] * inverse[i]
                for z in range(k, SUBLANES):
                    pivot[z][k] = pivot[z][k] - pivot[z][i] * weight
        if p + 1 < panels:
            divided = [new[i] * inverse[i] for i in span]
            update = []
            for m in span:
                line = divided[m]
                for i in range(m + 1, SUBLANES):
                    line = line + unit[i][m] * divided[i]
                update.append(line)
            for q in range(p + 1, panels):
                terms = [spread[q - p][m] * update[m] for m in span]
                while len(terms) > 1:
                    terms = [terms[a] + terms[a + 1] for a in range(0, len(terms), 2)]
                state[q] = state[q] - terms[0]
        panel = new[0] * lax.rsqrt(pivot[0][0])
        for i in range(1, SUBLANES):
            panel = jnp.where(sublane == i, new[i] * lax.rsqrt(pivot[i][i]), panel)
        out.append(panel)
    return jnp.concatenate(out, axis=0)[:, rank:]


def targets_kernel(total_items, parts, *refs):
    placed_ref, targets_ref = refs[parts:]
    gram = refs[0][...]
    for part in refs[1:parts]:
        gram = gram + part[...]
    rank = gram.shape[0]
    inverse = inverse_factor(gram) * math.sqrt(total_items)
    high = inverse.astype(jnp.bfloat16)
    low = (inverse - high.astype(jnp.float32)).astype(jnp.bfloat16)
    left = jnp.concatenate([high, high, low], axis=1)
    right = jnp.concatenate([placed_ref[...], placed_ref[:rank, :]], axis=0)
    targets_ref[...] = rank_dot(left, right, (1, 0))


def gram_parts(gram, mesh_size):
    if mesh_size & (mesh_size - 1):
        return [lax.psum(gram, AXES)]
    parts, step = [gram], 1
    while step < mesh_size:
        gram = sum(parts[1:], parts[0])
        parts = [gram, lax.ppermute(gram, AXES, [(i, i ^ (step | 1)) for i in range(mesh_size)])]
        step *= 2
    return parts


def body(mesh_size, affinity, old_basis, degrees, column_blocks, reorder):
    count, slots, block, _ = affinity.shape
    items, rank = old_basis.shape
    width = REACH * block
    edges = [b for b in range(count) if b < REACH or b >= count - REACH]
    affinity = in_vmem(affinity)
    basis = old_basis.T
    degree_rows = degrees.reshape(items // LANES, LANES)
    columns = column_blocks.T
    place = lax.axis_index(AXES).astype(jnp.int32).reshape(1)
    square = pltpu.VMEM((rank, rank), jnp.float32)

    near, far = pl.pallas_call(
        functools.partial(edges_kernel, width),
        out_shape=(pltpu.VMEM((rank, width), jnp.bfloat16),) * 2,
        in_specs=[SMEM, HBM, HBM],
        out_specs=(VMEM, VMEM),
        scratch_shapes=[
            pltpu.VMEM((2, rank, width), jnp.bfloat16),
            pltpu.VMEM(degree_rows.shape, jnp.int32),
            pltpu.SemaphoreType.DMA((3,)),
        ],
        compiler_params=PARAMS,
        cost_estimate=pl.CostEstimate(flops=1000 * affinity.size, bytes_accessed=40 * affinity.size, transcendentals=0),
        name="edges",
    )(place, in_hbm(basis), in_hbm(degree_rows))
    near = lax.ppermute(near, AXES, [(i, i ^ 1) for i in range(mesh_size) if i ^ 1 < mesh_size])
    crossing = range(1, mesh_size - 1, 2)
    far = lax.ppermute(far, AXES, [(i, i + 1) for i in crossing] + [(i + 1, i) for i in crossing])

    partial, inner, columns, degree_rows = pl.pallas_call(
        functools.partial(own_kernel, count, block, edges),
        out_shape=(
            pltpu.VMEM((rank, items), jnp.float32),
            square,
            pltpu.SMEM(columns.shape, jnp.int32),
            pltpu.VMEM(degree_rows.shape, jnp.int32),
        ),
        in_specs=[SMEM] + [HBM] * 3 + [VMEM],
        out_specs=(VMEM, VMEM, SMEM, VMEM),
        scratch_shapes=[
            pltpu.VMEM((count + 2 * REACH, rank, block), jnp.bfloat16),
            pltpu.VMEM((rank, items), jnp.bfloat16),
            pltpu.SemaphoreType.DMA((3,)),
        ],
        compiler_params=PARAMS,
        cost_estimate=pl.CostEstimate(
            flops=2 * count * slots * block * block * rank, bytes_accessed=0, transcendentals=0
        ),
        name="own",
    )(place, *map(in_hbm, (columns, basis, degree_rows)), affinity)

    outer, gram = pl.pallas_call(
        functools.partial(halo_kernel, count, block, edges),
        out_shape=(pltpu.VMEM((rank, len(edges) * block), jnp.float32), square),
        in_specs=[SMEM, SMEM] + [VMEM] * 6,
        out_specs=(VMEM, VMEM),
        scratch_shapes=[pltpu.VMEM((2 * REACH + 1, rank, block), jnp.bfloat16)],
        compiler_params=PARAMS,
        name="halo",
    )(place, columns, *map(in_vmem, (degree_rows, near, far)), affinity, *map(in_vmem, (partial, inner)))

    placed = pl.pallas_call(
        functools.partial(reorder_kernel, count, block, edges),
        out_shape=pltpu.VMEM((2 * rank, items), jnp.bfloat16),
        in_specs=[VMEM] * 3,
        out_specs=VMEM,
        compiler_params=PARAMS,
        cost_estimate=pl.CostEstimate(flops=4 * rank * items * block, bytes_accessed=0, transcendentals=0),
        name="reorder",
    )(in_vmem(partial), in_vmem(outer), in_vmem(reorder))

    parts = gram_parts(gram, mesh_size)
    targets = pl.pallas_call(
        functools.partial(targets_kernel, items * mesh_size, len(parts)),
        out_shape=jax.ShapeDtypeStruct((rank, items), jnp.float32),
        in_specs=[VMEM] * (len(parts) + 1),
        out_specs=VMEM,
        compiler_params=PARAMS,
        name="targets",
    )(*map(in_vmem, parts), in_vmem(placed))
    return targets.T


def solution(mesh):
    placed = (
        P(AXES, None, None, None),
        P(AXES, None),
        P(AXES),
        P(AXES, None),
        P(AXES, None),
    )
    mesh_size = mesh.shape["rows"] * mesh.shape["sub"]
    return jax.shard_map(
        functools.partial(body, mesh_size), mesh=mesh, in_specs=placed, out_specs=P(AXES, None), check_vma=False
    )
```

```python
import functools
import math

import jax
import jax.numpy as jnp
from jax import lax
from jax.experimental import pallas as pl
from jax.experimental.pallas import tpu as pltpu
from jax.sharding import PartitionSpec as P

REACH = 2
AXES = ("rows", "sub")
SUBLANES, LANES = 8, 128
CHUNKS = 4
VMEM = pl.BlockSpec(memory_space=pltpu.VMEM)
SMEM = pl.BlockSpec(memory_space=pltpu.SMEM)
HBM = pl.BlockSpec(memory_space=pltpu.HBM)
PARAMS = pltpu.CompilerParams(vmem_limit_bytes=16 << 20)


def in_vmem(x):
    return pltpu.with_memory_space_constraint(x, pltpu.VMEM)


def in_hbm(x):
    return pltpu.with_memory_space_constraint(x, pltpu.HBM)


def rank_dot(a, b, contract, precision=None):
    return lax.dot_general(
        a, b, ((contract[:1], contract[1:]), ((), ())), precision=precision, preferred_element_type=jnp.float32
    )


def gram_of(image):
    return rank_dot(image, image, (1, 1), lax.Precision.HIGHEST)


def inverse_root(degrees_ref, piece):
    return lax.rsqrt(degrees_ref[pl.ds(piece, 1), :].astype(jnp.float32))


def block_root(degrees_ref, b, block):
    pieces = block // LANES
    return jnp.concatenate([inverse_root(degrees_ref, b * pieces + c) for c in range(pieces)], axis=1)


def scaled_piece(basis_ref, degrees_ref, piece):
    columns = slice(piece * LANES, (piece + 1) * LANES)
    if not isinstance(piece, int):
        columns = pl.ds(pl.multiple_of(piece * LANES, LANES), LANES)
    return (inverse_root(degrees_ref, piece) * basis_ref[:, columns].astype(jnp.float32)).astype(jnp.bfloat16)


def edges_kernel(
    width, place_ref, columns_hbm, basis_hbm, degrees_hbm, far_ref, columns_ref, basis_ref, degrees_ref, sems
):
    pieces, last = width // LANES, (basis_ref.shape[1] - width) // LANES
    copies = [
        pltpu.make_async_copy(degrees_hbm, degrees_ref, sems.at[0]),
        pltpu.make_async_copy(basis_hbm, basis_ref, sems.at[1]),
        pltpu.make_async_copy(columns_hbm, columns_ref, sems.at[2]),
    ]
    for copy in copies:
        copy.start()
    odd = place_ref[0] % 2
    for copy in copies:
        copy.wait()
    for i in range(pieces):
        far_ref[:, i * LANES:(i + 1) * LANES] = scaled_piece(basis_ref, degrees_ref, odd * last + i)


def own_kernel(
    count, block, edges, place_ref, columns_ref, basis_ref, degrees_ref, affinity_ref, near_ref, partial_ref, gram_ref,
    extended
):
    pieces = block // LANES
    for b in range(REACH):
        extended[b] = jnp.zeros_like(extended[b])
        extended[count + REACH + b] = jnp.zeros_like(extended[b])
    for piece in range(count * pieces):
        b, c = divmod(piece, pieces)
        extended[REACH + b, :, c * LANES:(c + 1) * LANES] = scaled_piece(basis_ref, degrees_ref, piece)
    odd = place_ref[0] % 2
    for b in range(REACH):
        near_ref[:, b * block:(b + 1) * block] = extended[REACH + (1 - odd) * (count - REACH) + b]
    first = place_ref[0] * count - REACH
    inner = []
    for b in range(count):
        total = rank_dot(extended[REACH + b], affinity_ref[b, 0], (1, 1))
        for slot in range(1, affinity_ref.shape[1]):
            total += rank_dot(extended[columns_ref[slot, b] - first], affinity_ref[b, slot], (1, 1))
        if b not in edges:
            total *= block_root(degrees_ref, b, block)
            inner.append(total)
        partial_ref[:, b * block:(b + 1) * block] = total
    if inner:
        gram_ref[...] = gram_of(jnp.concatenate(inner, axis=1))
    else:
        gram_ref[...] = jnp.zeros_like(gram_ref)


def halo_kernel(
    count, block, edges, place_ref, columns_ref, degrees_ref, near_ref, far_ref, affinity_ref, partial_ref, inner_ref,
    image_ref, gram_ref, halo
):
    odd = place_ref[0] % 2
    for b in range(REACH):
        halo[(1 - odd) * REACH + b] = near_ref[:, b * block:(b + 1) * block]
        halo[odd * REACH + b] = far_ref[:, b * block:(b + 1) * block]
    halo[2 * REACH] = jnp.zeros_like(halo[0])
    first = place_ref[0] * count - REACH
    images = []
    for at, b in enumerate(edges):
        total = partial_ref[:, b * block:(b + 1) * block]
        for slot in range(1, affinity_ref.shape[1]):
            index = columns_ref[slot, b] - first
            index = jnp.where(index < REACH, index, jnp.where(index < REACH + count, 2 * REACH, index - count))
            total += rank_dot(halo[index], affinity_ref[b, slot], (1, 1))
        images.append(total * block_root(degrees_ref, b, block))
        image_ref[:, at * block:(at + 1) * block] = images[-1]
    gram_ref[...] = inner_ref[...] + gram_of(jnp.concatenate(images, axis=1))


def reorder_kernel(count, block, edges, inner_ref, outer_ref, reorder_ref, placed_ref):
    source = lax.broadcasted_iota(jnp.int32, (block, block), 0)
    for b in range(count):
        at = edges.index(b) if b in edges else b
        image = (outer_ref if b in edges else inner_ref)[:, at * block:(at + 1) * block]
        high = image.astype(jnp.bfloat16)
        low = (image - high.astype(jnp.float32)).astype(jnp.bfloat16)
        chosen = jnp.where(source == reorder_ref[b:b + 1, :], 1.0, 0.0).astype(jnp.bfloat16)
        moved = rank_dot(jnp.concatenate([high, low], axis=0), chosen, (1, 0))
        moved = moved.astype(jnp.bfloat16)
        rank = image.shape[0]
        placed_ref[:2 * rank, b * block:(b + 1) * block] = moved
        placed_ref[2 * rank:, b * block:(b + 1) * block] = moved[:rank]


def along_lanes(x, column):
    return jnp.broadcast_to(x[:, column:column + 1], (SUBLANES, LANES))


def along_sublanes(x, row):
    return jnp.broadcast_to(x[row:row + 1, :], (SUBLANES, LANES))


def inverse_factor(gram):
    rank = gram.shape[0]
    tiles, per = rank // SUBLANES, 2
    size = per * SUBLANES
    rows = lax.broadcasted_iota(jnp.int32, (rank, rank), 0)
    columns = lax.broadcasted_iota(jnp.int32, (rank, rank), 1)
    state = jnp.concatenate([gram, jnp.where(rows == columns, 1.0, 0.0)], axis=1)
    state = [state[SUBLANES * t:SUBLANES * (t + 1)] for t in range(tiles)]
    sublane = lax.broadcasted_iota(jnp.int32, (SUBLANES, LANES), 0)
    for top in range(0, tiles, per):
        at = top * SUBLANES
        live = [{t: along_lanes(state[t], at + j) for t in range(top, tiles)} for j in range(size)]
        diagonal = {}
        pivot = along_sublanes(live[0][top], 0)
        for i in range(size):
            tile, s = top + i // SUBLANES, i % SUBLANES
            inverse = 1.0 / pivot
            diagonal[tile] = jnp.where(sublane == s, pivot, diagonal[tile]) if s else pivot
            ahead = {j: along_sublanes(live[j][tile], s) for j in range(i + 1, size)}
            if ahead:
                tile_next, s_next = top + (i + 1) // SUBLANES, (i + 1) % SUBLANES
                pivot = along_sublanes(live[i + 1][tile_next], s_next) - along_sublanes(
                    live[i][tile_next], s_next
                ) * (ahead[i + 1] * inverse)
            row = along_sublanes(state[tile], s)
            for t in range(tile, tiles):
                column = live[i][t] * inverse
                for j in ahead:
                    live[j][t] = live[j][t] - column * ahead[j]
                if t == tile:
                    column = jnp.where(sublane > s, column, 0.0)
                state[t] = state[t] - column * row
        for t in range(top, top + per):
            state[t] = state[t] * lax.rsqrt(diagonal[t])
    return jnp.concatenate(state, axis=0)[:, rank:]


def targets_kernel(total_items, parts, *refs):
    placed_ref, targets_hbm, targets_ref, sems = refs[parts:]
    gram = refs[0][...]
    for part in refs[1:parts]:
        gram = gram + part[...]
    inverse = inverse_factor(gram) * math.sqrt(total_items)
    high = inverse.astype(jnp.bfloat16)
    low = (inverse - high.astype(jnp.float32)).astype(jnp.bfloat16)
    left = jnp.concatenate([high, high, low], axis=1)
    chunk = targets_ref.shape[1] // CHUNKS
    copies = []
    for c in range(CHUNKS):
        columns = slice(c * chunk, (c + 1) * chunk)
        targets_ref[:, columns] = rank_dot(left, placed_ref[:, columns], (1, 0))
        copies.append(pltpu.make_async_copy(targets_ref.at[:, columns], targets_hbm.at[:, columns], sems.at[c]))
        copies[-1].start()
    for copy in copies:
        copy.wait()


def gram_parts(gram, mesh_size):
    if mesh_size & (mesh_size - 1):
        return [lax.psum(gram, AXES)]
    bits = [1 << k for k in range(mesh_size.bit_length() - 2, 0, -1)]
    rounds = [[1]] + [[bit | 1] for bit in bits[:-2]]
    if bits:
        rounds.append([bit | 1 for bit in bits[:-3:-1]] + [sum(bits[-2:])] * (len(bits) > 1))
    parts = [gram]
    for masks in rounds:
        gram = sum(parts[1:], parts[0])
        parts = [gram] + [lax.ppermute(gram, AXES, [(i, i ^ mask) for i in range(mesh_size)]) for mask in masks]
    return parts


def body(mesh_size, affinity, old_basis, degrees, column_blocks, reorder):
    count, slots, block, _ = affinity.shape
    items, rank = old_basis.shape
    width = REACH * block
    edges = [b for b in range(count) if b < REACH or b >= count - REACH]
    affinity = in_vmem(affinity)
    basis = old_basis.T
    degree_rows = degrees.reshape(items // LANES, LANES)
    columns = column_blocks.T
    place = lax.axis_index(AXES).astype(jnp.int32).reshape(1)
    square = pltpu.VMEM((rank, rank), jnp.float32)

    far, columns, basis, degree_rows = pl.pallas_call(
        functools.partial(edges_kernel, width),
        out_shape=(
            pltpu.VMEM((rank, width), jnp.bfloat16),
            pltpu.SMEM(columns.shape, jnp.int32),
            pltpu.VMEM(basis.shape, jnp.bfloat16),
            pltpu.VMEM(degree_rows.shape, jnp.int32),
        ),
        in_specs=[SMEM, HBM, HBM, HBM],
        out_specs=(VMEM, SMEM, VMEM, VMEM),
        scratch_shapes=[pltpu.SemaphoreType.DMA((3,))],
        compiler_params=PARAMS,
        cost_estimate=pl.CostEstimate(flops=1000 * affinity.size, bytes_accessed=40 * affinity.size, transcendentals=0),
        name="edges",
    )(place, *map(in_hbm, (columns, basis, degree_rows)))
    crossing = range(1, mesh_size - 1, 2)
    far = lax.ppermute(far, AXES, [(i, i + 1) for i in crossing] + [(i + 1, i) for i in crossing])

    near, partial, inner = pl.pallas_call(
        functools.partial(own_kernel, count, block, edges),
        out_shape=(
            pltpu.VMEM((rank, width), jnp.bfloat16),
            pltpu.VMEM((rank, items), jnp.float32),
            square,
        ),
        in_specs=[SMEM, SMEM] + [VMEM] * 3,
        out_specs=(VMEM,) * 3,
        scratch_shapes=[pltpu.VMEM((count + 2 * REACH, rank, block), jnp.bfloat16)],
        compiler_params=PARAMS,
        cost_estimate=pl.CostEstimate(
            flops=2 * count * slots * block * block * rank, bytes_accessed=0, transcendentals=0
        ),
        name="own",
    )(place, columns, *map(in_vmem, (basis, degree_rows)), affinity)
    near = lax.ppermute(near, AXES, [(i, i ^ 1) for i in range(mesh_size) if i ^ 1 < mesh_size])

    outer, gram = pl.pallas_call(
        functools.partial(halo_kernel, count, block, edges),
        out_shape=(pltpu.VMEM((rank, len(edges) * block), jnp.float32), square),
        in_specs=[SMEM, SMEM] + [VMEM] * 6,
        out_specs=(VMEM, VMEM),
        scratch_shapes=[pltpu.VMEM((2 * REACH + 1, rank, block), jnp.bfloat16)],
        compiler_params=PARAMS,
        name="halo",
    )(place, columns, *map(in_vmem, (degree_rows, near, far)), affinity, *map(in_vmem, (partial, inner)))

    placed = pl.pallas_call(
        functools.partial(reorder_kernel, count, block, edges),
        out_shape=pltpu.VMEM((3 * rank, items), jnp.bfloat16),
        in_specs=[VMEM] * 3,
        out_specs=VMEM,
        compiler_params=PARAMS,
        cost_estimate=pl.CostEstimate(flops=4 * rank * items * block, bytes_accessed=0, transcendentals=0),
        name="reorder",
    )(in_vmem(partial), in_vmem(outer), in_vmem(reorder))

    parts = gram_parts(gram, mesh_size)
    targets = pl.pallas_call(
        functools.partial(targets_kernel, items * mesh_size, len(parts)),
        out_shape=jax.ShapeDtypeStruct((rank, items), jnp.float32),
        in_specs=[VMEM] * (len(parts) + 1),
        out_specs=HBM,
        scratch_shapes=[pltpu.VMEM((rank, items), jnp.float32), pltpu.SemaphoreType.DMA((CHUNKS,))],
        compiler_params=PARAMS,
        name="targets",
    )(*map(in_vmem, parts), in_vmem(placed))
    return targets.T


def solution(mesh):
    placed = (
        P(AXES, None, None, None),
        P(AXES, None),
        P(AXES),
        P(AXES, None),
        P(AXES, None),
    )
    mesh_size = mesh.shape["rows"] * mesh.shape["sub"]
    return jax.shard_map(
        functools.partial(body, mesh_size), mesh=mesh, in_specs=placed, out_specs=P(AXES, None), check_vma=False
    )
```

```python
import functools
import math

import jax
import jax.numpy as jnp
from jax import lax
from jax.experimental import pallas as pl
from jax.experimental.pallas import tpu as pltpu
from jax.sharding import PartitionSpec as P

REACH = 2
AXES = ("rows", "sub")
SUBLANES, LANES = 8, 128
CHUNKS = 4
VMEM = pl.BlockSpec(memory_space=pltpu.VMEM)
SMEM = pl.BlockSpec(memory_space=pltpu.SMEM)
HBM = pl.BlockSpec(memory_space=pltpu.HBM)
PARAMS = pltpu.CompilerParams(vmem_limit_bytes=16 << 20)


def in_vmem(x):
    return pltpu.with_memory_space_constraint(x, pltpu.VMEM)


def in_hbm(x):
    return pltpu.with_memory_space_constraint(x, pltpu.HBM)


def rank_dot(a, b, contract, precision=None):
    return lax.dot_general(
        a, b, ((contract[:1], contract[1:]), ((), ())), precision=precision, preferred_element_type=jnp.float32
    )


def gram_of(image):
    return rank_dot(image, image, (1, 1), lax.Precision.HIGHEST)


def inverse_root(degrees_ref, piece):
    return lax.rsqrt(degrees_ref[pl.ds(piece, 1), :].astype(jnp.float32))


def block_root(degrees_ref, b, block):
    pieces = block // LANES
    return jnp.concatenate([inverse_root(degrees_ref, b * pieces + c) for c in range(pieces)], axis=1)


def scaled_piece(basis_ref, degrees_ref, piece):
    columns = slice(piece * LANES, (piece + 1) * LANES)
    if not isinstance(piece, int):
        columns = pl.ds(pl.multiple_of(piece * LANES, LANES), LANES)
    return (inverse_root(degrees_ref, piece) * basis_ref[:, columns].astype(jnp.float32)).astype(jnp.bfloat16)


def edges_kernel(
    width, place_ref, columns_hbm, basis_hbm, degrees_hbm, far_ref, columns_ref, basis_ref, degrees_ref, sems
):
    pieces, last = width // LANES, (basis_ref.shape[1] - width) // LANES
    copies = [
        pltpu.make_async_copy(degrees_hbm, degrees_ref, sems.at[0]),
        pltpu.make_async_copy(basis_hbm, basis_ref, sems.at[1]),
        pltpu.make_async_copy(columns_hbm, columns_ref, sems.at[2]),
    ]
    for copy in copies:
        copy.start()
    odd = place_ref[0] % 2
    for copy in copies:
        copy.wait()
    for i in range(pieces):
        far_ref[:, i * LANES:(i + 1) * LANES] = scaled_piece(basis_ref, degrees_ref, odd * last + i)


def own_kernel(
    count, block, edges, place_ref, columns_ref, basis_ref, degrees_ref, affinity_ref, near_ref, partial_ref, gram_ref,
    extended
):
    pieces = block // LANES
    for b in range(REACH):
        extended[b] = jnp.zeros_like(extended[b])
        extended[count + REACH + b] = jnp.zeros_like(extended[b])
    for piece in range(count * pieces):
        b, c = divmod(piece, pieces)
        extended[REACH + b, :, c * LANES:(c + 1) * LANES] = scaled_piece(basis_ref, degrees_ref, piece)
    odd = place_ref[0] % 2
    for b in range(REACH):
        near_ref[:, b * block:(b + 1) * block] = extended[REACH + (1 - odd) * (count - REACH) + b]
    first = place_ref[0] * count - REACH
    inner = []
    for b in range(count):
        total = rank_dot(extended[REACH + b], affinity_ref[b, 0], (1, 1))
        for slot in range(1, affinity_ref.shape[1]):
            total += rank_dot(extended[columns_ref[slot, b] - first], affinity_ref[b, slot], (1, 1))
        if b not in edges:
            total *= block_root(degrees_ref, b, block)
            inner.append(total)
        partial_ref[:, b * block:(b + 1) * block] = total
    if inner:
        gram_ref[...] = gram_of(jnp.concatenate(inner, axis=1))
    else:
        gram_ref[...] = jnp.zeros_like(gram_ref)


def halo_kernel(
    count, block, edges, late, place_ref, columns_ref, degrees_ref, near_ref, rest_ref, most_ref, affinity_ref, partial_ref,
    own_gram_ref, image_ref, gram_ref, halo
):
    odd = place_ref[0] % 2
    is_late = (place_ref[0] == late[0]) | (place_ref[0] == late[1])
    for b in range(REACH):
        columns = slice(b * block, (b + 1) * block)
        halo[(1 - odd) * REACH + b] = near_ref[:, columns]
        halo[odd * REACH + b] = jnp.where(is_late, rest_ref[:, columns], most_ref[:, columns])
    halo[2 * REACH] = jnp.zeros_like(halo[0])
    first = place_ref[0] * count - REACH
    images = []
    for at, b in enumerate(edges):
        total = partial_ref[:, b * block:(b + 1) * block]
        for slot in range(1, affinity_ref.shape[1]):
            index = columns_ref[slot, b] - first
            index = jnp.where(index < REACH, index, jnp.where(index < REACH + count, 2 * REACH, index - count))
            total += rank_dot(halo[index], affinity_ref[b, slot], (1, 1))
        images.append(total * block_root(degrees_ref, b, block))
        image_ref[:, at * block:(at + 1) * block] = images[-1]
    gram = own_gram_ref[...] + gram_of(jnp.concatenate(images, axis=1))
    half = gram.shape[0] // 2
    gram_ref[...] = jnp.concatenate([gram[:half], gram[half:]], axis=1)


def reorder_kernel(count, block, edges, inner_ref, outer_ref, reorder_ref, placed_ref):
    source = lax.broadcasted_iota(jnp.int32, (block, block), 0)
    for b in range(count):
        at = edges.index(b) if b in edges else b
        image = (outer_ref if b in edges else inner_ref)[:, at * block:(at + 1) * block]
        high = image.astype(jnp.bfloat16)
        low = (image - high.astype(jnp.float32)).astype(jnp.bfloat16)
        chosen = jnp.where(source == reorder_ref[b:b + 1, :], 1.0, 0.0).astype(jnp.bfloat16)
        moved = rank_dot(jnp.concatenate([high, low], axis=0), chosen, (1, 0))
        moved = moved.astype(jnp.bfloat16)
        rank = image.shape[0]
        placed_ref[:2 * rank, b * block:(b + 1) * block] = moved
        placed_ref[2 * rank:, b * block:(b + 1) * block] = moved[:rank]


def along_lanes(x, column):
    return jnp.broadcast_to(x[:, column:column + 1], (SUBLANES, LANES))


def along_sublanes(x, row):
    return jnp.broadcast_to(x[row:row + 1, :], (SUBLANES, LANES))


def inverse_factor(folded):
    rank = folded.shape[1] // 2
    tiles, per = rank // SUBLANES, 2
    size = per * SUBLANES
    rows = lax.broadcasted_iota(jnp.int32, (rank, 2 * rank), 0)
    columns = lax.broadcasted_iota(jnp.int32, (rank, 2 * rank), 1)
    state = jnp.concatenate([folded, pltpu.roll(folded, rank, 1)], axis=0)
    state = jnp.where(columns < rank, state, jnp.where(columns - rank == rows, 1.0, 0.0))
    state = [state[SUBLANES * t:SUBLANES * (t + 1)] for t in range(tiles)]
    sublane = lax.broadcasted_iota(jnp.int32, (SUBLANES, LANES), 0)
    for top in range(0, tiles, per):
        at = top * SUBLANES
        live = [{t: along_lanes(state[t], at + j) for t in range(top, tiles)} for j in range(size)]
        diagonal = {}
        pivot = along_sublanes(live[0][top], 0)
        for i in range(size):
            tile, s = top + i // SUBLANES, i % SUBLANES
            inverse = 1.0 / pivot
            diagonal[tile] = jnp.where(sublane == s, pivot, diagonal[tile]) if s else pivot
            ahead = {j: along_sublanes(live[j][tile], s) for j in range(i + 1, size)}
            if ahead:
                tile_next, s_next = top + (i + 1) // SUBLANES, (i + 1) % SUBLANES
                pivot = along_sublanes(live[i + 1][tile_next], s_next) - along_sublanes(
                    live[i][tile_next], s_next
                ) * (ahead[i + 1] * inverse)
            row = along_sublanes(state[tile], s)
            for t in range(tile, tiles):
                column = live[i][t] * inverse
                for j in ahead:
                    live[j][t] = live[j][t] - column * ahead[j]
                if t == tile:
                    column = jnp.where(sublane > s, column, 0.0)
                state[t] = state[t] - column * row
        for t in range(top, top + per):
            state[t] = state[t] * lax.rsqrt(diagonal[t])
    return jnp.concatenate(state, axis=0)[:, rank:]


def targets_kernel(total_items, parts, *refs):
    placed_ref, targets_hbm, targets_ref, sems = refs[parts:]
    gram = refs[0][...]
    for part in refs[1:parts]:
        gram = gram + part[...]
    inverse = inverse_factor(gram) * math.sqrt(total_items)
    high = inverse.astype(jnp.bfloat16)
    low = (inverse - high.astype(jnp.float32)).astype(jnp.bfloat16)
    left = jnp.concatenate([high, high, low], axis=1)
    chunk = targets_ref.shape[1] // CHUNKS
    copies = []
    for c in range(CHUNKS):
        columns = slice(c * chunk, (c + 1) * chunk)
        targets_ref[:, columns] = rank_dot(left, placed_ref[:, columns], (1, 0))
        copies.append(pltpu.make_async_copy(targets_ref.at[:, columns], targets_hbm.at[:, columns], sems.at[c]))
        copies[-1].start()
    for copy in copies:
        copy.wait()


def gram_parts(gram, mesh_size):
    if mesh_size & (mesh_size - 1):
        return [lax.psum(gram, AXES)]
    bits = [1 << k for k in range(mesh_size.bit_length() - 2, 0, -1)]
    rounds = [[1]] + [[bit | 1] for bit in bits[:-2]]
    if bits:
        rounds.append([bit | 1 for bit in bits[:-3:-1]] + [sum(bits[-2:])] * (len(bits) > 1))
    parts = [gram]
    for masks in rounds:
        gram = sum(parts[1:], parts[0])
        parts = [gram] + [lax.ppermute(gram, AXES, [(i, i ^ mask) for i in range(mesh_size)]) for mask in masks]
    return parts


def cycle(*devices):
    return list(zip(devices, devices[1:] + devices[:1]))


def crossing_pairs(mesh_size):
    n = mesh_size
    if n % 2 or n < 8:
        pairs = [pair for i in range(1, n - 1, 2) for pair in cycle(i, i + 1)]
        return [pairs, pairs]
    most = [pair for i in range(3, n - 4, 2) for pair in cycle(i, i + 1)]
    most += cycle(2, 1, 0) + cycle(n - 3, n - 2, n - 1)
    rest = [pair for i in range(4, n - 4, 2) for pair in cycle(i, i + 1)]
    rest += cycle(1, 2, 3, 0) + cycle(n - 2, n - 3, n - 4, n - 1)
    return [rest, most]


def body(mesh_size, affinity, old_basis, degrees, column_blocks, reorder):
    count, slots, block, _ = affinity.shape
    items, rank = old_basis.shape
    width = REACH * block
    edges = [b for b in range(count) if b < REACH or b >= count - REACH]
    affinity = in_vmem(affinity)
    basis = old_basis.T
    degree_rows = degrees.reshape(items // LANES, LANES)
    columns = column_blocks.T
    place = lax.axis_index(AXES).astype(jnp.int32).reshape(1)
    folded = pltpu.VMEM((rank // 2, 2 * rank), jnp.float32)

    far, columns, basis, degree_rows = pl.pallas_call(
        functools.partial(edges_kernel, width),
        out_shape=(
            pltpu.VMEM((rank, width), jnp.bfloat16),
            pltpu.SMEM(columns.shape, jnp.int32),
            pltpu.VMEM(basis.shape, jnp.bfloat16),
            pltpu.VMEM(degree_rows.shape, jnp.int32),
        ),
        in_specs=[SMEM, HBM, HBM, HBM],
        out_specs=(VMEM, SMEM, VMEM, VMEM),
        scratch_shapes=[pltpu.SemaphoreType.DMA((3,))],
        compiler_params=PARAMS,
        cost_estimate=pl.CostEstimate(flops=1000 * affinity.size, bytes_accessed=40 * affinity.size, transcendentals=0),
        name="edges",
    )(place, *map(in_hbm, (columns, basis, degree_rows)))
    distant = [lax.ppermute(far, AXES, pairs) for pairs in crossing_pairs(mesh_size)]

    near, partial, inner = pl.pallas_call(
        functools.partial(own_kernel, count, block, edges),
        out_shape=(
            pltpu.VMEM((rank, width), jnp.bfloat16),
            pltpu.VMEM((rank, items), jnp.float32),
            pltpu.VMEM((rank, rank), jnp.float32),
        ),
        in_specs=[SMEM, SMEM] + [VMEM] * 3,
        out_specs=(VMEM,) * 3,
        scratch_shapes=[pltpu.VMEM((count + 2 * REACH, rank, block), jnp.bfloat16)],
        compiler_params=PARAMS,
        cost_estimate=pl.CostEstimate(
            flops=2 * count * slots * block * block * rank, bytes_accessed=0, transcendentals=0
        ),
        name="own",
    )(place, columns, *map(in_vmem, (basis, degree_rows)), affinity)
    near = lax.ppermute(near, AXES, [(i, i ^ 1) for i in range(mesh_size) if i ^ 1 < mesh_size])

    outer, gram = pl.pallas_call(
        functools.partial(halo_kernel, count, block, edges, (2, mesh_size - 3)),
        out_shape=(pltpu.VMEM((rank, len(edges) * block), jnp.float32), folded),
        in_specs=[SMEM, SMEM] + [VMEM] * 7,
        out_specs=(VMEM, VMEM),
        scratch_shapes=[pltpu.VMEM((2 * REACH + 1, rank, block), jnp.bfloat16)],
        compiler_params=PARAMS,
        name="halo",
    )(place, columns, *map(in_vmem, (degree_rows, near, *distant)), affinity, *map(in_vmem, (partial, inner)))

    placed = pl.pallas_call(
        functools.partial(reorder_kernel, count, block, edges),
        out_shape=pltpu.VMEM((3 * rank, items), jnp.bfloat16),
        in_specs=[VMEM] * 3,
        out_specs=VMEM,
        compiler_params=PARAMS,
        cost_estimate=pl.CostEstimate(flops=4 * rank * items * block, bytes_accessed=0, transcendentals=0),
        name="reorder",
    )(in_vmem(partial), in_vmem(outer), in_vmem(reorder))

    parts = gram_parts(gram, mesh_size)
    targets = pl.pallas_call(
        functools.partial(targets_kernel, items * mesh_size, len(parts)),
        out_shape=jax.ShapeDtypeStruct((rank, items), jnp.float32),
        in_specs=[VMEM] * (len(parts) + 1),
        out_specs=HBM,
        scratch_shapes=[pltpu.VMEM((rank, items), jnp.float32), pltpu.SemaphoreType.DMA((CHUNKS,))],
        compiler_params=PARAMS,
        name="targets",
    )(*map(in_vmem, parts), in_vmem(placed))
    return targets.T


def solution(mesh):
    placed = (
        P(AXES, None, None, None),
        P(AXES, None),
        P(AXES),
        P(AXES, None),
        P(AXES, None),
    )
    mesh_size = mesh.shape["rows"] * mesh.shape["sub"]
    return jax.shard_map(
        functools.partial(body, mesh_size), mesh=mesh, in_specs=placed, out_specs=P(AXES, None), check_vma=False
    )
```

```python
import functools
import math

import jax
import jax.numpy as jnp
from jax import lax
from jax.experimental import pallas as pl
from jax.experimental.pallas import tpu as pltpu
from jax.sharding import PartitionSpec as P

REACH = 2
AXES = ("rows", "sub")
SUBLANES, LANES = 8, 128
CHUNKS = 4
VMEM = pl.BlockSpec(memory_space=pltpu.VMEM)
SMEM = pl.BlockSpec(memory_space=pltpu.SMEM)
HBM = pl.BlockSpec(memory_space=pltpu.HBM)
PARAMS = pltpu.CompilerParams(vmem_limit_bytes=16 << 20)


def in_vmem(x):
    return pltpu.with_memory_space_constraint(x, pltpu.VMEM)


def in_hbm(x):
    return pltpu.with_memory_space_constraint(x, pltpu.HBM)


def rank_dot(a, b, contract, precision=None):
    return lax.dot_general(
        a, b, ((contract[:1], contract[1:]), ((), ())), precision=precision, preferred_element_type=jnp.float32
    )


def split(x):
    high = x.astype(jnp.bfloat16)
    return jnp.concatenate([high, (x - high.astype(jnp.float32)).astype(jnp.bfloat16)], axis=0)


def gram_halves(terms):
    rank = terms.shape[0] // 2
    whole = rank_dot(terms, terms, (1, 1))
    return whole[:rank] + whole[rank:]


def inverse_root(degrees_ref, piece):
    return lax.rsqrt(degrees_ref[pl.ds(piece, 1), :].astype(jnp.float32))


def block_root(degrees_ref, b, block):
    pieces = block // LANES
    return jnp.concatenate([inverse_root(degrees_ref, b * pieces + c) for c in range(pieces)], axis=1)


def scaled(degrees_ref, piece, basis):
    return (inverse_root(degrees_ref, piece) * basis.astype(jnp.float32)).astype(jnp.bfloat16)


def edges_kernel(
    width, place_ref, columns_hbm, basis_hbm, degrees_hbm, far_ref, columns_ref, basis_ref, degrees_ref, edge_ref, sems
):
    odd = place_ref[0] % 2
    last = basis_hbm.shape[1] - width
    edge_hbm = basis_hbm.at[:, pl.ds(pl.multiple_of(odd * last, LANES), width)]
    copies = [
        pltpu.make_async_copy(edge_hbm, edge_ref, sems.at[0]),
        pltpu.make_async_copy(degrees_hbm, degrees_ref, sems.at[1]),
        pltpu.make_async_copy(basis_hbm, basis_ref, sems.at[2]),
        pltpu.make_async_copy(columns_hbm, columns_ref, sems.at[3]),
    ]
    for copy in copies:
        copy.start()
    for copy in copies[:2]:
        copy.wait()
    for i in range(width // LANES):
        columns = slice(i * LANES, (i + 1) * LANES)
        far_ref[:, columns] = scaled(degrees_ref, odd * (last // LANES) + i, edge_ref[:, columns])
    for copy in copies[2:]:
        copy.wait()


def own_kernel(
    count, block, edges, place_ref, columns_ref, basis_ref, degrees_ref, affinity_ref, near_ref, partial_ref, gram_ref,
    extended
):
    pieces = block // LANES
    for b in range(REACH):
        extended[b] = jnp.zeros_like(extended[b])
        extended[count + REACH + b] = jnp.zeros_like(extended[b])
    for piece in range(count * pieces):
        b, c = divmod(piece, pieces)
        basis = basis_ref[:, piece * LANES:(piece + 1) * LANES]
        extended[REACH + b, :, c * LANES:(c + 1) * LANES] = scaled(degrees_ref, piece, basis)
    odd = place_ref[0] % 2
    for b in range(REACH):
        near_ref[:, b * block:(b + 1) * block] = extended[REACH + (1 - odd) * (count - REACH) + b]
    first = place_ref[0] * count - REACH
    inner = []
    for b in range(count):
        total = rank_dot(extended[REACH + b], affinity_ref[b, 0], (1, 1))
        for slot in range(1, affinity_ref.shape[1]):
            total += rank_dot(extended[columns_ref[slot, b] - first], affinity_ref[b, slot], (1, 1))
        if b not in edges:
            total *= block_root(degrees_ref, b, block)
            inner.append(split(total))
        partial_ref[:, b * block:(b + 1) * block] = total
    if inner:
        gram_ref[...] = gram_halves(jnp.concatenate(inner, axis=1))
    else:
        gram_ref[...] = jnp.zeros_like(gram_ref)


def halo_kernel(
    count, block, edges, late, place_ref, columns_ref, degrees_ref, near_ref, rest_ref, most_ref, affinity_ref, partial_ref,
    own_gram_ref, image_ref, gram_ref, halo
):
    odd = place_ref[0] % 2
    is_late = (place_ref[0] == late[0]) | (place_ref[0] == late[1])
    for b in range(REACH):
        columns = slice(b * block, (b + 1) * block)
        halo[(1 - odd) * REACH + b] = near_ref[:, columns]
        halo[odd * REACH + b] = jnp.where(is_late, rest_ref[:, columns], most_ref[:, columns])
    halo[2 * REACH] = jnp.zeros_like(halo[0])
    first = place_ref[0] * count - REACH
    images = []
    for at, b in enumerate(edges):
        total = partial_ref[:, b * block:(b + 1) * block]
        for slot in range(1, affinity_ref.shape[1]):
            index = columns_ref[slot, b] - first
            index = jnp.where(index < REACH, index, jnp.where(index < REACH + count, 2 * REACH, index - count))
            total += rank_dot(halo[index], affinity_ref[b, slot], (1, 1))
        images.append(split(total * block_root(degrees_ref, b, block)))
        image_ref[:, at * block:(at + 1) * block] = images[-1]
    halves = own_gram_ref[...] + gram_halves(jnp.concatenate(images, axis=1))
    rank = halves.shape[0]
    halves = halves + pltpu.roll(halves, rank, 1)
    lane = lax.broadcasted_iota(jnp.int32, gram_ref.shape, 1)
    gram_ref[...] = jnp.where(lane < rank, halves[:rank // 2], halves[rank // 2:])


def reorder_kernel(count, block, edges, inner_ref, outer_ref, reorder_ref, placed_ref):
    source = lax.broadcasted_iota(jnp.int32, (block, block), 0)
    for b in range(count):
        at = edges.index(b) if b in edges else b
        columns = slice(at * block, (at + 1) * block)
        terms = outer_ref[:, columns] if b in edges else split(inner_ref[:, columns])
        chosen = jnp.where(source == reorder_ref[b:b + 1, :], 1.0, 0.0).astype(jnp.bfloat16)
        moved = rank_dot(terms, chosen, (1, 0))
        moved = moved.astype(jnp.bfloat16)
        rank = terms.shape[0] // 2
        placed_ref[:2 * rank, b * block:(b + 1) * block] = moved
        placed_ref[2 * rank:, b * block:(b + 1) * block] = moved[:rank]


def along_lanes(x, column):
    return jnp.broadcast_to(x[:, column:column + 1], (SUBLANES, LANES))


def along_sublanes(x, row):
    return jnp.broadcast_to(x[row:row + 1, :], (SUBLANES, LANES))


def inverse_factor(folded):
    rank = folded.shape[1] // 2
    tiles, per = rank // SUBLANES, 2
    size = per * SUBLANES
    rows = lax.broadcasted_iota(jnp.int32, (rank, 2 * rank), 0)
    columns = lax.broadcasted_iota(jnp.int32, (rank, 2 * rank), 1)
    state = jnp.concatenate([folded, pltpu.roll(folded, rank, 1)], axis=0)
    state = jnp.where(columns < rank, state, jnp.where(columns - rank == rows, 1.0, 0.0))
    state = [state[SUBLANES * t:SUBLANES * (t + 1)] for t in range(tiles)]
    sublane = lax.broadcasted_iota(jnp.int32, (SUBLANES, LANES), 0)
    for top in range(0, tiles, per):
        at = top * SUBLANES
        live = [{t: along_lanes(state[t], at + j) for t in range(top, tiles)} for j in range(size)]
        diagonal = {}
        pivot = along_sublanes(live[0][top], 0)
        for i in range(size):
            tile, s = top + i // SUBLANES, i % SUBLANES
            inverse = 1.0 / pivot
            diagonal[tile] = jnp.where(sublane == s, pivot, diagonal[tile]) if s else pivot
            ahead = {j: along_sublanes(live[j][tile], s) for j in range(i + 1, size)}
            if ahead:
                tile_next, s_next = top + (i + 1) // SUBLANES, (i + 1) % SUBLANES
                pivot = along_sublanes(live[i + 1][tile_next], s_next) - along_sublanes(
                    live[i][tile_next], s_next
                ) * (ahead[i + 1] * inverse)
            row = along_sublanes(state[tile], s)
            for t in range(tile, tiles):
                column = live[i][t] * inverse
                for j in ahead:
                    live[j][t] = live[j][t] - column * ahead[j]
                if t == tile:
                    column = jnp.where(sublane > s, column, 0.0)
                state[t] = state[t] - column * row
        for t in range(top, top + per):
            state[t] = state[t] * lax.rsqrt(diagonal[t])
    return jnp.concatenate(state, axis=0)


def targets_kernel(total_items, parts, *refs):
    placed_ref, targets_hbm, targets_ref, sems = refs[parts:]
    gram = refs[0][...]
    for part in refs[1:parts]:
        gram = gram + part[...]
    right = inverse_factor(gram) * math.sqrt(total_items)
    rank = right.shape[0]
    left = pltpu.roll(right, rank, 1)
    lane = lax.broadcasted_iota(jnp.int32, right.shape, 1)
    high = jnp.where(lane < rank, left, right).astype(jnp.bfloat16)
    low = (left - left.astype(jnp.bfloat16).astype(jnp.float32)).astype(jnp.bfloat16)
    left = jnp.concatenate([high, low[:, :rank]], axis=1)
    chunk = targets_ref.shape[1] // CHUNKS
    copies = []
    for c in range(CHUNKS):
        columns = slice(c * chunk, (c + 1) * chunk)
        targets_ref[:, columns] = rank_dot(left, placed_ref[:, columns], (1, 0))
        copies.append(pltpu.make_async_copy(targets_ref.at[:, columns], targets_hbm.at[:, columns], sems.at[c]))
        copies[-1].start()
    for copy in copies:
        copy.wait()


def gram_parts(gram, mesh_size):
    if mesh_size & (mesh_size - 1):
        return [lax.psum(gram, AXES)]
    bits = [1 << k for k in range(mesh_size.bit_length() - 2, 0, -1)]
    rounds = [[1]] + [[bit | 1] for bit in bits[:-2]]
    if bits:
        rounds.append([bit | 1 for bit in bits[:-3:-1]] + [sum(bits[-2:])] * (len(bits) > 1))
    parts = [gram]
    for masks in rounds:
        gram = sum(parts[1:], parts[0])
        parts = [gram] + [lax.ppermute(gram, AXES, [(i, i ^ mask) for i in range(mesh_size)]) for mask in masks]
    return parts


def cycle(*devices):
    return list(zip(devices, devices[1:] + devices[:1]))


def crossing_pairs(mesh_size):
    n = mesh_size
    if n % 2 or n < 8:
        pairs = [pair for i in range(1, n - 1, 2) for pair in cycle(i, i + 1)]
        return [pairs, pairs]
    most = [pair for i in range(3, n - 4, 2) for pair in cycle(i, i + 1)]
    most += cycle(2, 1, 0) + cycle(n - 3, n - 2, n - 1)
    rest = [pair for i in range(4, n - 4, 2) for pair in cycle(i, i + 1)]
    rest += cycle(1, 2, 3, 0) + cycle(n - 2, n - 3, n - 4, n - 1)
    return [rest, most]


def body(mesh_size, affinity, old_basis, degrees, column_blocks, reorder):
    count, slots, block, _ = affinity.shape
    items, rank = old_basis.shape
    width = REACH * block
    edges = [b for b in range(count) if b < REACH or b >= count - REACH]
    affinity = in_vmem(affinity)
    basis = old_basis.T
    degree_rows = degrees.reshape(items // LANES, LANES)
    columns = column_blocks.T
    place = lax.axis_index(AXES).astype(jnp.int32).reshape(1)
    folded = pltpu.VMEM((rank // 2, 2 * rank), jnp.float32)

    far, columns, basis, degree_rows = pl.pallas_call(
        functools.partial(edges_kernel, width),
        out_shape=(
            pltpu.VMEM((rank, width), jnp.bfloat16),
            pltpu.SMEM(columns.shape, jnp.int32),
            pltpu.VMEM(basis.shape, jnp.bfloat16),
            pltpu.VMEM(degree_rows.shape, jnp.int32),
        ),
        in_specs=[SMEM, HBM, HBM, HBM],
        out_specs=(VMEM, SMEM, VMEM, VMEM),
        scratch_shapes=[pltpu.VMEM((rank, width), jnp.bfloat16), pltpu.SemaphoreType.DMA((4,))],
        compiler_params=PARAMS,
        cost_estimate=pl.CostEstimate(flops=1000 * affinity.size, bytes_accessed=40 * affinity.size, transcendentals=0),
        name="edges",
    )(place, *map(in_hbm, (columns, basis, degree_rows)))
    distant = [lax.ppermute(far, AXES, pairs) for pairs in crossing_pairs(mesh_size)]

    near, partial, inner = pl.pallas_call(
        functools.partial(own_kernel, count, block, edges),
        out_shape=(
            pltpu.VMEM((rank, width), jnp.bfloat16),
            pltpu.VMEM((rank, items), jnp.float32),
            pltpu.VMEM((rank, 2 * rank), jnp.float32),
        ),
        in_specs=[SMEM, SMEM] + [VMEM] * 3,
        out_specs=(VMEM,) * 3,
        scratch_shapes=[pltpu.VMEM((count + 2 * REACH, rank, block), jnp.bfloat16)],
        compiler_params=PARAMS,
        cost_estimate=pl.CostEstimate(
            flops=2 * count * slots * block * block * rank, bytes_accessed=0, transcendentals=0
        ),
        name="own",
    )(place, columns, *map(in_vmem, (basis, degree_rows)), affinity)
    near = lax.ppermute(near, AXES, [(i, i ^ 1) for i in range(mesh_size) if i ^ 1 < mesh_size])

    outer, gram = pl.pallas_call(
        functools.partial(halo_kernel, count, block, edges, (2, mesh_size - 3)),
        out_shape=(pltpu.VMEM((2 * rank, len(edges) * block), jnp.bfloat16), folded),
        in_specs=[SMEM, SMEM] + [VMEM] * 7,
        out_specs=(VMEM, VMEM),
        scratch_shapes=[pltpu.VMEM((2 * REACH + 1, rank, block), jnp.bfloat16)],
        compiler_params=PARAMS,
        name="halo",
    )(place, columns, *map(in_vmem, (degree_rows, near, *distant)), affinity, *map(in_vmem, (partial, inner)))

    placed = pl.pallas_call(
        functools.partial(reorder_kernel, count, block, edges),
        out_shape=pltpu.VMEM((3 * rank, items), jnp.bfloat16),
        in_specs=[VMEM] * 3,
        out_specs=VMEM,
        compiler_params=PARAMS,
        cost_estimate=pl.CostEstimate(flops=4 * rank * items * block, bytes_accessed=0, transcendentals=0),
        name="reorder",
    )(in_vmem(partial), in_vmem(outer), in_vmem(reorder))

    parts = gram_parts(gram, mesh_size)
    targets = pl.pallas_call(
        functools.partial(targets_kernel, items * mesh_size, len(parts)),
        out_shape=jax.ShapeDtypeStruct((rank, items), jnp.float32),
        in_specs=[VMEM] * (len(parts) + 1),
        out_specs=HBM,
        scratch_shapes=[pltpu.VMEM((rank, items), jnp.float32), pltpu.SemaphoreType.DMA((CHUNKS,))],
        compiler_params=PARAMS,
        name="targets",
    )(*map(in_vmem, parts), in_vmem(placed))
    return targets.T


def solution(mesh):
    placed = (
        P(AXES, None, None, None),
        P(AXES, None),
        P(AXES),
        P(AXES, None),
        P(AXES, None),
    )
    mesh_size = mesh.shape["rows"] * mesh.shape["sub"]
    return jax.shard_map(
        functools.partial(body, mesh_size), mesh=mesh, in_specs=placed, out_specs=P(AXES, None), check_vma=False
    )
```

```python
import functools
import math

import jax
import jax.numpy as jnp
from jax import lax
from jax.experimental import pallas as pl
from jax.experimental.pallas import tpu as pltpu
from jax.sharding import PartitionSpec as P

REACH = 2
AXES = ("rows", "sub")
SUBLANES, LANES = 8, 128
CHUNKS = 4
VMEM = pl.BlockSpec(memory_space=pltpu.VMEM)
SMEM = pl.BlockSpec(memory_space=pltpu.SMEM)
HBM = pl.BlockSpec(memory_space=pltpu.HBM)
PARAMS = pltpu.CompilerParams(vmem_limit_bytes=16 << 20)


def in_vmem(x):
    return pltpu.with_memory_space_constraint(x, pltpu.VMEM)


def in_hbm(x):
    return pltpu.with_memory_space_constraint(x, pltpu.HBM)


def rank_dot(a, b, contract, precision=None):
    return lax.dot_general(
        a, b, ((contract[:1], contract[1:]), ((), ())), precision=precision, preferred_element_type=jnp.float32
    )


def split(x):
    high = x.astype(jnp.bfloat16)
    return jnp.concatenate([high, (x - high.astype(jnp.float32)).astype(jnp.bfloat16)], axis=0)


def gram_halves(terms):
    rank = terms.shape[0] // 2
    whole = rank_dot(terms, terms, (1, 1))
    return whole[:rank] + whole[rank:]


def inverse_root(degrees_ref, piece):
    return lax.rsqrt(degrees_ref[pl.ds(piece, 1), :].astype(jnp.float32))


def block_root(degrees_ref, b, block):
    pieces = block // LANES
    return jnp.concatenate([inverse_root(degrees_ref, b * pieces + c) for c in range(pieces)], axis=1)


def scaled(degrees_ref, piece, basis):
    return (inverse_root(degrees_ref, piece) * basis.astype(jnp.float32)).astype(jnp.bfloat16)


def edges_kernel(
    width, place_ref, columns_hbm, basis_hbm, degrees_hbm, far_ref, columns_ref, basis_ref, degrees_ref, edge_ref, sems
):
    odd = place_ref[0] % 2
    last = basis_hbm.shape[1] - width
    edge_hbm = basis_hbm.at[:, pl.ds(pl.multiple_of(odd * last, LANES), width)]
    copies = [
        pltpu.make_async_copy(edge_hbm, edge_ref, sems.at[0]),
        pltpu.make_async_copy(degrees_hbm, degrees_ref, sems.at[1]),
        pltpu.make_async_copy(basis_hbm, basis_ref, sems.at[2]),
        pltpu.make_async_copy(columns_hbm, columns_ref, sems.at[3]),
    ]
    for copy in copies:
        copy.start()
    for copy in copies[:2]:
        copy.wait()
    for i in range(width // LANES):
        columns = slice(i * LANES, (i + 1) * LANES)
        far_ref[:, columns] = scaled(degrees_ref, odd * (last // LANES) + i, edge_ref[:, columns])
    for copy in copies[2:]:
        copy.wait()


def own_kernel(count, block, edges, place_ref, columns_ref, basis_ref, degrees_ref, affinity_ref, *refs):
    near_refs, (partial_ref, gram_ref, extended) = refs[:REACH], refs[REACH:]
    pieces = block // LANES
    for b in range(REACH):
        extended[b] = jnp.zeros_like(extended[b])
        extended[count + REACH + b] = jnp.zeros_like(extended[b])
    for piece in range(count * pieces):
        b, c = divmod(piece, pieces)
        basis = basis_ref[:, piece * LANES:(piece + 1) * LANES]
        extended[REACH + b, :, c * LANES:(c + 1) * LANES] = scaled(degrees_ref, piece, basis)
    odd = place_ref[0] % 2
    for b in range(REACH):
        near_refs[b][...] = extended[REACH + (1 - odd) * (count - REACH) + b]
    first = place_ref[0] * count - REACH
    inner = []
    for b in range(count):
        total = rank_dot(extended[REACH + b], affinity_ref[b, 0], (1, 1))
        for slot in range(1, affinity_ref.shape[1]):
            total += rank_dot(extended[columns_ref[slot, b] - first], affinity_ref[b, slot], (1, 1))
        if b not in edges:
            total *= block_root(degrees_ref, b, block)
            inner.append(split(total))
        partial_ref[:, b * block:(b + 1) * block] = total
    if inner:
        gram_ref[...] = gram_halves(jnp.concatenate(inner, axis=1))
    else:
        gram_ref[...] = jnp.zeros_like(gram_ref)


def side_images(count, block, left, place_ref, columns_ref, degrees_ref, affinity_ref, partial_ref, halo):
    start = jnp.where(left, 0, count - REACH)
    first = place_ref[0] * count - REACH
    pieces = block // LANES
    images = []
    for b in range(REACH):
        row = start + b
        total = partial_ref[:, pl.ds(pl.multiple_of(row * block, block), block)]
        for slot in range(1, affinity_ref.shape[1]):
            index = columns_ref[slot, row] - first
            index = jnp.where(index < REACH, index, jnp.where(index < REACH + count, REACH, index - REACH - count))
            total += rank_dot(halo[index], affinity_ref[row, slot], (1, 1))
        root = [inverse_root(degrees_ref, row * pieces + c) for c in range(pieces)]
        images.append(split(total * jnp.concatenate(root, axis=1)))
    return jnp.concatenate(images, axis=1)


def near_kernel(count, block, place_ref, columns_ref, degrees_ref, *refs):
    near_refs, (affinity_ref, partial_ref, own_gram_ref, image_ref, gram_ref, halo) = refs[:REACH], refs[REACH:]
    for b in range(REACH):
        halo[b] = near_refs[b][...]
    halo[REACH] = jnp.zeros_like(halo[0])
    left = place_ref[0] % 2 == 1
    image = side_images(count, block, left, place_ref, columns_ref, degrees_ref, affinity_ref, partial_ref, halo)
    image_ref[...] = image
    gram_ref[...] = own_gram_ref[...] + gram_halves(image)


def far_kernel(
    count, block, late, place_ref, columns_ref, degrees_ref, rest_ref, most_ref, affinity_ref, partial_ref, near_gram_ref,
    image_ref, gram_ref, halo
):
    is_late = (place_ref[0] == late[0]) | (place_ref[0] == late[1])
    for b in range(REACH):
        columns = slice(b * block, (b + 1) * block)
        halo[b] = jnp.where(is_late, rest_ref[:, columns], most_ref[:, columns])
    halo[REACH] = jnp.zeros_like(halo[0])
    left = place_ref[0] % 2 == 0
    image = side_images(count, block, left, place_ref, columns_ref, degrees_ref, affinity_ref, partial_ref, halo)
    image_ref[...] = image
    halves = near_gram_ref[...] + gram_halves(image)
    rank = halves.shape[0]
    halves = halves + pltpu.roll(halves, rank, 1)
    lane = lax.broadcasted_iota(jnp.int32, gram_ref.shape, 1)
    gram_ref[...] = jnp.where(lane < rank, halves[:rank // 2], halves[rank // 2:])


def reorder_kernel(count, block, edges, place_ref, inner_ref, near_ref, far_ref, reorder_ref, placed_ref):
    odd = place_ref[0] % 2 == 1
    source = lax.broadcasted_iota(jnp.int32, (block, block), 0)
    for b in range(count):
        if b in edges:
            columns = slice(b % REACH * block, (b % REACH + 1) * block)
            nearer = odd if b < REACH else ~odd
            terms = jnp.where(nearer, near_ref[:, columns], far_ref[:, columns])
        else:
            terms = split(inner_ref[:, b * block:(b + 1) * block])
        chosen = jnp.where(source == reorder_ref[b:b + 1, :], 1.0, 0.0).astype(jnp.bfloat16)
        moved = rank_dot(terms, chosen, (1, 0))
        moved = moved.astype(jnp.bfloat16)
        rank = terms.shape[0] // 2
        placed_ref[:2 * rank, b * block:(b + 1) * block] = moved
        placed_ref[2 * rank:, b * block:(b + 1) * block] = moved[:rank]


def along_lanes(x, column):
    return jnp.broadcast_to(x[:, column:column + 1], (SUBLANES, LANES))


def along_sublanes(x, row):
    return jnp.broadcast_to(x[row:row + 1, :], (SUBLANES, LANES))


def inverse_factor(folded):
    rank = folded.shape[1] // 2
    tiles, per = rank // SUBLANES, 2
    size = per * SUBLANES
    rows = lax.broadcasted_iota(jnp.int32, (rank, 2 * rank), 0)
    columns = lax.broadcasted_iota(jnp.int32, (rank, 2 * rank), 1)
    state = jnp.concatenate([folded, pltpu.roll(folded, rank, 1)], axis=0)
    state = jnp.where(columns < rank, state, jnp.where(columns - rank == rows, 1.0, 0.0))
    state = [state[SUBLANES * t:SUBLANES * (t + 1)] for t in range(tiles)]
    sublane = lax.broadcasted_iota(jnp.int32, (SUBLANES, LANES), 0)
    for top in range(0, tiles, per):
        at = top * SUBLANES
        live = [{t: along_lanes(state[t], at + j) for t in range(top, tiles)} for j in range(size)]
        diagonal = {}
        pivot = along_sublanes(live[0][top], 0)
        for i in range(size):
            tile, s = top + i // SUBLANES, i % SUBLANES
            inverse = 1.0 / pivot
            diagonal[tile] = jnp.where(sublane == s, pivot, diagonal[tile]) if s else pivot
            ahead = {j: along_sublanes(live[j][tile], s) for j in range(i + 1, size)}
            if ahead:
                tile_next, s_next = top + (i + 1) // SUBLANES, (i + 1) % SUBLANES
                pivot = along_sublanes(live[i + 1][tile_next], s_next) - along_sublanes(
                    live[i][tile_next], s_next
                ) * (ahead[i + 1] * inverse)
            row = along_sublanes(state[tile], s)
            for t in range(tile, tiles):
                column = live[i][t] * inverse
                for j in ahead:
                    live[j][t] = live[j][t] - column * ahead[j]
                if t == tile:
                    column = jnp.where(sublane > s, column, 0.0)
                state[t] = state[t] - column * row
        for t in range(top, top + per):
            state[t] = state[t] * lax.rsqrt(diagonal[t])
    return jnp.concatenate(state, axis=0)


def targets_kernel(total_items, parts, *refs):
    placed_ref, targets_hbm, targets_ref, sems = refs[parts:]
    gram = refs[0][...]
    for part in refs[1:parts]:
        gram = gram + part[...]
    right = inverse_factor(gram) * math.sqrt(total_items)
    rank = right.shape[0]
    left = pltpu.roll(right, rank, 1)
    lane = lax.broadcasted_iota(jnp.int32, right.shape, 1)
    high = jnp.where(lane < rank, left, right).astype(jnp.bfloat16)
    low = (left - left.astype(jnp.bfloat16).astype(jnp.float32)).astype(jnp.bfloat16)
    left = jnp.concatenate([high, low[:, :rank]], axis=1)
    chunk = targets_ref.shape[1] // CHUNKS
    copies = []
    for c in range(CHUNKS):
        columns = slice(c * chunk, (c + 1) * chunk)
        targets_ref[:, columns] = rank_dot(left, placed_ref[:, columns], (1, 0))
        copies.append(pltpu.make_async_copy(targets_ref.at[:, columns], targets_hbm.at[:, columns], sems.at[c]))
        copies[-1].start()
    for copy in copies:
        copy.wait()


def gram_parts(gram, mesh_size):
    if mesh_size & (mesh_size - 1):
        return [lax.psum(gram, AXES)]
    bits = [1 << k for k in range(1, mesh_size.bit_length() - 1)]
    rounds = [[1]] + [[bit | 1] for bit in bits[2:]]
    if bits:
        rounds.append([bit | 1 for bit in bits[1::-1]] + [sum(bits[:2]) | 1] * (len(bits) > 1))
    parts = [gram]
    for masks in rounds:
        gram = sum(parts[1:], parts[0])
        parts = [gram] + [lax.ppermute(gram, AXES, [(i, i ^ mask) for i in range(mesh_size)]) for mask in masks]
    return parts


def cycle(*devices):
    return list(zip(devices, devices[1:] + devices[:1]))


def crossing_pairs(mesh_size):
    n = mesh_size
    if n % 2 or n < 8:
        pairs = [pair for i in range(1, n - 1, 2) for pair in cycle(i, i + 1)]
        return [pairs, pairs]
    most = [pair for i in range(3, n - 4, 2) for pair in cycle(i, i + 1)]
    most += cycle(2, 1, 0) + cycle(n - 3, n - 2, n - 1)
    rest = [pair for i in range(4, n - 4, 2) for pair in cycle(i, i + 1)]
    rest += cycle(1, 2, 3, 0) + cycle(n - 2, n - 3, n - 4, n - 1)
    return [rest, most]


def body(mesh_size, affinity, old_basis, degrees, column_blocks, reorder):
    count, slots, block, _ = affinity.shape
    items, rank = old_basis.shape
    width = REACH * block
    assert count % REACH == 0 and count >= 2 * REACH
    edges = [b for b in range(count) if b < REACH or b >= count - REACH]
    affinity = in_vmem(affinity)
    basis = old_basis.T
    degree_rows = degrees.reshape(items // LANES, LANES)
    columns = column_blocks.T
    place = lax.axis_index(AXES).astype(jnp.int32).reshape(1)
    folded = pltpu.VMEM((rank // 2, 2 * rank), jnp.float32)

    far, columns, basis, degree_rows = pl.pallas_call(
        functools.partial(edges_kernel, width),
        out_shape=(
            pltpu.VMEM((rank, width), jnp.bfloat16),
            pltpu.SMEM(columns.shape, jnp.int32),
            pltpu.VMEM(basis.shape, jnp.bfloat16),
            pltpu.VMEM(degree_rows.shape, jnp.int32),
        ),
        in_specs=[SMEM, HBM, HBM, HBM],
        out_specs=(VMEM, SMEM, VMEM, VMEM),
        scratch_shapes=[pltpu.VMEM((rank, width), jnp.bfloat16), pltpu.SemaphoreType.DMA((4,))],
        compiler_params=PARAMS,
        cost_estimate=pl.CostEstimate(flops=1000 * affinity.size, bytes_accessed=40 * affinity.size, transcendentals=0),
        name="edges",
    )(place, *map(in_hbm, (columns, basis, degree_rows)))
    distant = [lax.ppermute(far, AXES, pairs) for pairs in crossing_pairs(mesh_size)]

    *near, partial, inner = pl.pallas_call(
        functools.partial(own_kernel, count, block, edges),
        out_shape=(
            *[pltpu.VMEM((rank, block), jnp.bfloat16)] * REACH,
            pltpu.VMEM((rank, items), jnp.float32),
            pltpu.VMEM((rank, 2 * rank), jnp.float32),
        ),
        in_specs=[SMEM, SMEM] + [VMEM] * 3,
        out_specs=(VMEM,) * (2 + REACH),
        scratch_shapes=[pltpu.VMEM((count + 2 * REACH, rank, block), jnp.bfloat16)],
        compiler_params=PARAMS,
        cost_estimate=pl.CostEstimate(
            flops=2 * count * slots * block * block * rank, bytes_accessed=0, transcendentals=0
        ),
        name="own",
    )(place, columns, *map(in_vmem, (basis, degree_rows)), affinity)
    near = [lax.ppermute(x, AXES, [(i, i ^ 1) for i in range(mesh_size) if i ^ 1 < mesh_size]) for x in near]

    side = dict(
        out_specs=(VMEM, VMEM),
        scratch_shapes=[pltpu.VMEM((REACH + 1, rank, block), jnp.bfloat16)],
        compiler_params=PARAMS,
        cost_estimate=pl.CostEstimate(flops=1, bytes_accessed=1, transcendentals=0),
    )
    side_image = pltpu.VMEM((2 * rank, width), jnp.bfloat16)
    near_image, gram = pl.pallas_call(
        functools.partial(near_kernel, count, block),
        out_shape=(side_image, pltpu.VMEM((rank, 2 * rank), jnp.float32)),
        in_specs=[SMEM, SMEM] + [VMEM] * (4 + REACH),
        name="near",
        **side,
    )(place, columns, *map(in_vmem, (degree_rows, *near)), affinity, *map(in_vmem, (partial, inner)))
    far_image, gram = pl.pallas_call(
        functools.partial(far_kernel, count, block, (2, mesh_size - 3)),
        out_shape=(side_image, folded),
        in_specs=[SMEM, SMEM] + [VMEM] * 6,
        name="far",
        **side,
    )(place, columns, *map(in_vmem, (degree_rows, *distant)), affinity, *map(in_vmem, (partial, gram)))

    placed = pl.pallas_call(
        functools.partial(reorder_kernel, count, block, edges),
        out_shape=pltpu.VMEM((3 * rank, items), jnp.bfloat16),
        in_specs=[SMEM] + [VMEM] * 4,
        out_specs=VMEM,
        compiler_params=PARAMS,
        cost_estimate=pl.CostEstimate(flops=4 * rank * items * block, bytes_accessed=0, transcendentals=0),
        name="reorder",
    )(place, *map(in_vmem, (partial, near_image, far_image, reorder)))

    parts = gram_parts(gram, mesh_size)
    targets = pl.pallas_call(
        functools.partial(targets_kernel, items * mesh_size, len(parts)),
        out_shape=jax.ShapeDtypeStruct((rank, items), jnp.float32),
        in_specs=[VMEM] * (len(parts) + 1),
        out_specs=HBM,
        scratch_shapes=[pltpu.VMEM((rank, items), jnp.float32), pltpu.SemaphoreType.DMA((CHUNKS,))],
        compiler_params=PARAMS,
        name="targets",
    )(*map(in_vmem, parts), in_vmem(placed))
    return targets.T


def solution(mesh):
    placed = (
        P(AXES, None, None, None),
        P(AXES, None),
        P(AXES),
        P(AXES, None),
        P(AXES, None),
    )
    mesh_size = mesh.shape["rows"] * mesh.shape["sub"]
    return jax.shard_map(
        functools.partial(body, mesh_size), mesh=mesh, in_specs=placed, out_specs=P(AXES, None), check_vma=False
    )
```

```python
import functools
import math

import jax
import jax.numpy as jnp
from jax import lax
from jax.experimental import pallas as pl
from jax.experimental.pallas import tpu as pltpu
from jax.sharding import PartitionSpec as P

REACH = 2
AXES = ("rows", "sub")
SUBLANES, LANES = 8, 128
CHUNKS = 4
VMEM = pl.BlockSpec(memory_space=pltpu.VMEM)
SMEM = pl.BlockSpec(memory_space=pltpu.SMEM)
HBM = pl.BlockSpec(memory_space=pltpu.HBM)
PARAMS = pltpu.CompilerParams(vmem_limit_bytes=16 << 20)


def in_vmem(x):
    return pltpu.with_memory_space_constraint(x, pltpu.VMEM)


def in_hbm(x):
    return pltpu.with_memory_space_constraint(x, pltpu.HBM)


def rank_dot(a, b, contract, precision=None):
    return lax.dot_general(
        a, b, ((contract[:1], contract[1:]), ((), ())), precision=precision, preferred_element_type=jnp.float32
    )


def split(x):
    high = x.astype(jnp.bfloat16)
    return jnp.concatenate([high, (x - high.astype(jnp.float32)).astype(jnp.bfloat16)], axis=0)


def gram_halves(terms):
    rank = terms.shape[0] // 2
    whole = rank_dot(terms, terms, (1, 1))
    return whole[:rank] + whole[rank:]


def inverse_root(degrees_ref, piece):
    return lax.rsqrt(degrees_ref[pl.ds(piece, 1), :].astype(jnp.float32))


def block_root(degrees_ref, b, block):
    pieces = block // LANES
    return jnp.concatenate([inverse_root(degrees_ref, b * pieces + c) for c in range(pieces)], axis=1)


def scaled(degrees_ref, piece, basis):
    return (inverse_root(degrees_ref, piece) * basis.astype(jnp.float32)).astype(jnp.bfloat16)


def edges_kernel(
    width, place_ref, columns_hbm, basis_hbm, degrees_hbm, far_ref, columns_ref, basis_ref, degrees_ref, edge_ref, sems
):
    odd = place_ref[0] % 2
    last = basis_hbm.shape[1] - width
    edge_hbm = basis_hbm.at[:, pl.ds(pl.multiple_of(odd * last, LANES), width)]
    copies = [
        pltpu.make_async_copy(edge_hbm, edge_ref, sems.at[0]),
        pltpu.make_async_copy(degrees_hbm, degrees_ref, sems.at[1]),
        pltpu.make_async_copy(basis_hbm, basis_ref, sems.at[2]),
        pltpu.make_async_copy(columns_hbm, columns_ref, sems.at[3]),
    ]
    for copy in copies:
        copy.start()
    for copy in copies[:2]:
        copy.wait()
    for i in range(width // LANES):
        columns = slice(i * LANES, (i + 1) * LANES)
        far_ref[:, columns] = scaled(degrees_ref, odd * (last // LANES) + i, edge_ref[:, columns])
    for copy in copies[2:]:
        copy.wait()


def own_kernel(count, block, edges, place_ref, columns_ref, basis_ref, degrees_ref, affinity_ref, *refs):
    near_refs, (partial_ref, gram_ref, extended) = refs[:REACH], refs[REACH:]
    pieces = block // LANES
    for b in range(REACH):
        extended[b] = jnp.zeros_like(extended[b])
        extended[count + REACH + b] = jnp.zeros_like(extended[b])
    for piece in range(count * pieces):
        b, c = divmod(piece, pieces)
        basis = basis_ref[:, piece * LANES:(piece + 1) * LANES]
        extended[REACH + b, :, c * LANES:(c + 1) * LANES] = scaled(degrees_ref, piece, basis)
    odd = place_ref[0] % 2
    for b in range(REACH):
        near_refs[b][...] = extended[REACH + (1 - odd) * (count - REACH) + b]
    first = place_ref[0] * count - REACH
    inner = []
    for b in range(count):
        total = rank_dot(extended[REACH + b], affinity_ref[b, 0], (1, 1))
        for slot in range(1, affinity_ref.shape[1]):
            total += rank_dot(extended[columns_ref[slot, b] - first], affinity_ref[b, slot], (1, 1))
        if b not in edges:
            total *= block_root(degrees_ref, b, block)
            inner.append(split(total))
        partial_ref[:, b * block:(b + 1) * block] = total
    if inner:
        gram_ref[...] = gram_halves(jnp.concatenate(inner, axis=1))
    else:
        gram_ref[...] = jnp.zeros_like(gram_ref)


def side_images(count, block, left, place_ref, columns_ref, degrees_ref, affinity_ref, partial_ref, halo):
    first = place_ref[0] * count - REACH
    pieces = block // LANES
    slots = affinity_ref.shape[1]
    images = []
    for r in range(REACH):
        row = jnp.where(left, r, count - 1 - r)
        total = partial_ref[:, pl.ds(pl.multiple_of(row * block, block), block)]
        named = [columns_ref[slot, row] - first for slot in range(slots)]
        beyond = [(index < REACH) | (index >= REACH + count) for index in named]
        picks = [(slot, named[slot], beyond[slot]) for slot in range(1, slots)]
        if REACH - r == 1:
            slot, index, outside = picks[0]
            for other, other_index, other_outside in picks[1:]:
                slot, index = jnp.where(other_outside, other, slot), jnp.where(other_outside, other_index, index)
                outside = outside | other_outside
            picks = [(slot, index, outside)]
        for slot, index, outside in picks:
            index = jnp.where(outside, jnp.where(index < REACH, index, index - REACH - count), REACH)
            total += rank_dot(halo[index], affinity_ref[row, slot], (1, 1))
        root = [inverse_root(degrees_ref, row * pieces + c) for c in range(pieces)]
        images.append(split(total * jnp.concatenate(root, axis=1)))
    placed = [jnp.where(left, near, far) for near, far in zip(images, images[::-1])]
    return jnp.concatenate(images, axis=1), jnp.concatenate(placed, axis=1)


def near_kernel(count, block, place_ref, columns_ref, degrees_ref, *refs):
    near_refs, (affinity_ref, partial_ref, own_gram_ref, image_ref, gram_ref, halo) = refs[:REACH], refs[REACH:]
    for b in range(REACH):
        halo[b] = near_refs[b][...]
    halo[REACH] = jnp.zeros_like(halo[0])
    left = place_ref[0] % 2 == 1
    image, placed = side_images(count, block, left, place_ref, columns_ref, degrees_ref, affinity_ref, partial_ref, halo)
    image_ref[...] = placed
    gram_ref[...] = own_gram_ref[...] + gram_halves(image)


def far_kernel(
    count, block, late, place_ref, columns_ref, degrees_ref, rest_ref, most_ref, affinity_ref, partial_ref, near_gram_ref,
    image_ref, gram_ref, halo
):
    is_late = (place_ref[0] == late[0]) | (place_ref[0] == late[1])
    for b in range(REACH):
        columns = slice(b * block, (b + 1) * block)
        halo[b] = jnp.where(is_late, rest_ref[:, columns], most_ref[:, columns])
    halo[REACH] = jnp.zeros_like(halo[0])
    left = place_ref[0] % 2 == 0
    image, placed = side_images(count, block, left, place_ref, columns_ref, degrees_ref, affinity_ref, partial_ref, halo)
    image_ref[...] = placed
    halves = near_gram_ref[...] + gram_halves(image)
    rank = halves.shape[0]
    halves = halves + pltpu.roll(halves, rank, 1)
    lane = lax.broadcasted_iota(jnp.int32, gram_ref.shape, 1)
    gram_ref[...] = jnp.where(lane < rank, halves[:rank // 2], halves[rank // 2:])


def reorder_kernel(count, block, edges, place_ref, inner_ref, near_ref, far_ref, reorder_ref, placed_ref):
    odd = place_ref[0] % 2 == 1
    source = lax.broadcasted_iota(jnp.int32, (block, block), 0)
    for b in range(count):
        if b in edges:
            columns = slice(b % REACH * block, (b % REACH + 1) * block)
            nearer = odd if b < REACH else ~odd
            terms = jnp.where(nearer, near_ref[:, columns], far_ref[:, columns])
        else:
            terms = split(inner_ref[:, b * block:(b + 1) * block])
        chosen = jnp.where(source == reorder_ref[b:b + 1, :], 1.0, 0.0).astype(jnp.bfloat16)
        moved = rank_dot(terms, chosen, (1, 0))
        moved = moved.astype(jnp.bfloat16)
        rank = terms.shape[0] // 2
        placed_ref[:2 * rank, b * block:(b + 1) * block] = moved
        placed_ref[2 * rank:, b * block:(b + 1) * block] = moved[:rank]


def along_lanes(x, column):
    return jnp.broadcast_to(x[:, column:column + 1], (SUBLANES, LANES))


def along_sublanes(x, row):
    return jnp.broadcast_to(x[row:row + 1, :], (SUBLANES, LANES))


def inverse_factor(folded):
    rank = folded.shape[1] // 2
    tiles, per = rank // SUBLANES, 2
    size = per * SUBLANES
    rows = lax.broadcasted_iota(jnp.int32, (rank, 2 * rank), 0)
    columns = lax.broadcasted_iota(jnp.int32, (rank, 2 * rank), 1)
    state = jnp.concatenate([folded, pltpu.roll(folded, rank, 1)], axis=0)
    state = jnp.where(columns < rank, state, jnp.where(columns - rank == rows, 1.0, 0.0))
    state = [state[SUBLANES * t:SUBLANES * (t + 1)] for t in range(tiles)]
    sublane = lax.broadcasted_iota(jnp.int32, (SUBLANES, LANES), 0)
    for top in range(0, tiles, per):
        at = top * SUBLANES
        live = [{t: along_lanes(state[t], at + j) for t in range(top, tiles)} for j in range(size)]
        diagonal = {}
        pivot = along_sublanes(live[0][top], 0)
        for i in range(size):
            tile, s = top + i // SUBLANES, i % SUBLANES
            inverse = 1.0 / pivot
            diagonal[tile] = jnp.where(sublane == s, pivot, diagonal[tile]) if s else pivot
            ahead = {j: along_sublanes(live[j][tile], s) for j in range(i + 1, size)}
            if ahead:
                tile_next, s_next = top + (i + 1) // SUBLANES, (i + 1) % SUBLANES
                pivot = along_sublanes(live[i + 1][tile_next], s_next) - along_sublanes(
                    live[i][tile_next], s_next
                ) * (ahead[i + 1] * inverse)
            row = along_sublanes(state[tile], s)
            for t in range(tile, tiles):
                column = live[i][t] * inverse
                for j in ahead:
                    live[j][t] = live[j][t] - column * ahead[j]
                if t == tile:
                    column = jnp.where(sublane > s, column, 0.0)
                state[t] = state[t] - column * row
        for t in range(top, top + per):
            state[t] = state[t] * lax.rsqrt(diagonal[t])
    return jnp.concatenate(state, axis=0)


def targets_kernel(total_items, parts, *refs):
    placed_ref, targets_hbm, targets_ref, sems = refs[parts:]
    gram = refs[0][...]
    for part in refs[1:parts]:
        gram = gram + part[...]
    right = inverse_factor(gram) * math.sqrt(total_items)
    rank = right.shape[0]
    left = pltpu.roll(right, rank, 1)
    lane = lax.broadcasted_iota(jnp.int32, right.shape, 1)
    high = jnp.where(lane < rank, left, right).astype(jnp.bfloat16)
    low = (left - left.astype(jnp.bfloat16).astype(jnp.float32)).astype(jnp.bfloat16)
    left = jnp.concatenate([high, low[:, :rank]], axis=1)
    chunk = targets_ref.shape[1] // CHUNKS
    copies = []
    for c in range(CHUNKS):
        columns = slice(c * chunk, (c + 1) * chunk)
        targets_ref[:, columns] = rank_dot(left, placed_ref[:, columns], (1, 0))
        copies.append(pltpu.make_async_copy(targets_ref.at[:, columns], targets_hbm.at[:, columns], sems.at[c]))
        copies[-1].start()
    for copy in copies:
        copy.wait()


def gram_parts(gram, mesh_size):
    if mesh_size & (mesh_size - 1):
        return [lax.psum(gram, AXES)]
    bits = [1 << k for k in range(1, mesh_size.bit_length() - 1)]
    rounds = [[1]] + [[bit | 1] for bit in bits[2:]]
    if bits:
        rounds.append([bit | 1 for bit in bits[1::-1]] + [sum(bits[:2]) | 1] * (len(bits) > 1))
    parts = [gram]
    for masks in rounds:
        gram = sum(parts[1:], parts[0])
        parts = [gram] + [lax.ppermute(gram, AXES, [(i, i ^ mask) for i in range(mesh_size)]) for mask in masks]
    return parts


def cycle(*devices):
    return list(zip(devices, devices[1:] + devices[:1]))


def crossing_pairs(mesh_size):
    n = mesh_size
    if n % 2 or n < 8:
        pairs = [pair for i in range(1, n - 1, 2) for pair in cycle(i, i + 1)]
        return [pairs, pairs]
    most = [pair for i in range(3, n - 4, 2) for pair in cycle(i, i + 1)]
    most += cycle(2, 1, 0) + cycle(n - 3, n - 2, n - 1)
    rest = [pair for i in range(4, n - 4, 2) for pair in cycle(i, i + 1)]
    rest += cycle(1, 2, 3, 0) + cycle(n - 2, n - 3, n - 4, n - 1)
    return [rest, most]


def body(mesh_size, affinity, old_basis, degrees, column_blocks, reorder):
    count, slots, block, _ = affinity.shape
    items, rank = old_basis.shape
    width = REACH * block
    assert count % REACH == 0 and count >= 2 * REACH
    edges = [b for b in range(count) if b < REACH or b >= count - REACH]
    affinity = in_vmem(affinity)
    basis = old_basis.T
    degree_rows = degrees.reshape(items // LANES, LANES)
    columns = column_blocks.T
    place = lax.axis_index(AXES).astype(jnp.int32).reshape(1)
    folded = pltpu.VMEM((rank // 2, 2 * rank), jnp.float32)

    far, columns, basis, degree_rows = pl.pallas_call(
        functools.partial(edges_kernel, width),
        out_shape=(
            pltpu.VMEM((rank, width), jnp.bfloat16),
            pltpu.SMEM(columns.shape, jnp.int32),
            pltpu.VMEM(basis.shape, jnp.bfloat16),
            pltpu.VMEM(degree_rows.shape, jnp.int32),
        ),
        in_specs=[SMEM, HBM, HBM, HBM],
        out_specs=(VMEM, SMEM, VMEM, VMEM),
        scratch_shapes=[pltpu.VMEM((rank, width), jnp.bfloat16), pltpu.SemaphoreType.DMA((4,))],
        compiler_params=PARAMS,
        cost_estimate=pl.CostEstimate(flops=1000 * affinity.size, bytes_accessed=40 * affinity.size, transcendentals=0),
        name="edges",
    )(place, *map(in_hbm, (columns, basis, degree_rows)))
    distant = [lax.ppermute(far, AXES, pairs) for pairs in crossing_pairs(mesh_size)]

    *near, partial, inner = pl.pallas_call(
        functools.partial(own_kernel, count, block, edges),
        out_shape=(
            *[pltpu.VMEM((rank, block), jnp.bfloat16)] * REACH,
            pltpu.VMEM((rank, items), jnp.float32),
            pltpu.VMEM((rank, 2 * rank), jnp.float32),
        ),
        in_specs=[SMEM, SMEM] + [VMEM] * 3,
        out_specs=(VMEM,) * (2 + REACH),
        scratch_shapes=[pltpu.VMEM((count + 2 * REACH, rank, block), jnp.bfloat16)],
        compiler_params=PARAMS,
        cost_estimate=pl.CostEstimate(
            flops=2 * count * slots * block * block * rank, bytes_accessed=0, transcendentals=0
        ),
        name="own",
    )(place, columns, *map(in_vmem, (basis, degree_rows)), affinity)
    near = [lax.ppermute(x, AXES, [(i, i ^ 1) for i in range(mesh_size) if i ^ 1 < mesh_size]) for x in near]

    side = dict(
        out_specs=(VMEM, VMEM),
        scratch_shapes=[pltpu.VMEM((REACH + 1, rank, block), jnp.bfloat16)],
        compiler_params=PARAMS,
        cost_estimate=pl.CostEstimate(flops=1, bytes_accessed=1, transcendentals=0),
    )
    side_image = pltpu.VMEM((2 * rank, width), jnp.bfloat16)
    near_image, gram = pl.pallas_call(
        functools.partial(near_kernel, count, block),
        out_shape=(side_image, pltpu.VMEM((rank, 2 * rank), jnp.float32)),
        in_specs=[SMEM, SMEM] + [VMEM] * (4 + REACH),
        name="near",
        **side,
    )(place, columns, *map(in_vmem, (degree_rows, *near)), affinity, *map(in_vmem, (partial, inner)))
    far_image, gram = pl.pallas_call(
        functools.partial(far_kernel, count, block, (2, mesh_size - 3)),
        out_shape=(side_image, folded),
        in_specs=[SMEM, SMEM] + [VMEM] * 6,
        name="far",
        **side,
    )(place, columns, *map(in_vmem, (degree_rows, *distant)), affinity, *map(in_vmem, (partial, gram)))

    placed = pl.pallas_call(
        functools.partial(reorder_kernel, count, block, edges),
        out_shape=pltpu.VMEM((3 * rank, items), jnp.bfloat16),
        in_specs=[SMEM] + [VMEM] * 4,
        out_specs=VMEM,
        compiler_params=PARAMS,
        cost_estimate=pl.CostEstimate(flops=4 * rank * items * block, bytes_accessed=0, transcendentals=0),
        name="reorder",
    )(place, *map(in_vmem, (partial, near_image, far_image, reorder)))

    parts = gram_parts(gram, mesh_size)
    targets = pl.pallas_call(
        functools.partial(targets_kernel, items * mesh_size, len(parts)),
        out_shape=jax.ShapeDtypeStruct((rank, items), jnp.float32),
        in_specs=[VMEM] * (len(parts) + 1),
        out_specs=HBM,
        scratch_shapes=[pltpu.VMEM((rank, items), jnp.float32), pltpu.SemaphoreType.DMA((CHUNKS,))],
        compiler_params=PARAMS,
        name="targets",
    )(*map(in_vmem, parts), in_vmem(placed))
    return targets.T


def solution(mesh):
    placed = (
        P(AXES, None, None, None),
        P(AXES, None),
        P(AXES),
        P(AXES, None),
        P(AXES, None),
    )
    mesh_size = mesh.shape["rows"] * mesh.shape["sub"]
    return jax.shard_map(
        functools.partial(body, mesh_size), mesh=mesh, in_specs=placed, out_specs=P(AXES, None), check_vma=False
    )
```

```python
import functools
import math

import jax
import jax.numpy as jnp
from jax import lax
from jax.experimental import pallas as pl
from jax.experimental.pallas import tpu as pltpu
from jax.sharding import PartitionSpec as P

REACH = 2
AXES = ("rows", "sub")
SUBLANES, LANES = 8, 128
CHUNKS = 4
VMEM = pl.BlockSpec(memory_space=pltpu.VMEM)
SMEM = pl.BlockSpec(memory_space=pltpu.SMEM)
HBM = pl.BlockSpec(memory_space=pltpu.HBM)
PARAMS = pltpu.CompilerParams(vmem_limit_bytes=16 << 20)


def in_vmem(x):
    return pltpu.with_memory_space_constraint(x, pltpu.VMEM)


def in_hbm(x):
    return pltpu.with_memory_space_constraint(x, pltpu.HBM)


def rank_dot(a, b, contract, precision=None):
    return lax.dot_general(
        a, b, ((contract[:1], contract[1:]), ((), ())), precision=precision, preferred_element_type=jnp.float32
    )


def split(x):
    high = x.astype(jnp.bfloat16)
    return jnp.concatenate([high, (x - high.astype(jnp.float32)).astype(jnp.bfloat16)], axis=0)


def gram_halves(terms):
    rank = terms.shape[0] // 2
    whole = rank_dot(terms, terms, (1, 1))
    return whole[:rank] + whole[rank:]


def inverse_root(degrees_ref, piece):
    return lax.rsqrt(degrees_ref[pl.ds(piece, 1), :].astype(jnp.float32))


def block_root(degrees_ref, b, block):
    pieces = block // LANES
    return jnp.concatenate([inverse_root(degrees_ref, b * pieces + c) for c in range(pieces)], axis=1)


def scaled(degrees_ref, piece, basis):
    return (inverse_root(degrees_ref, piece) * basis.astype(jnp.float32)).astype(jnp.bfloat16)


def edges_kernel(
    width, place_ref, columns_hbm, basis_hbm, degrees_hbm, far_ref, columns_ref, basis_ref, degrees_ref, edge_ref, sems
):
    odd = place_ref[0] % 2
    last = basis_hbm.shape[1] - width
    edge_hbm = basis_hbm.at[:, pl.ds(pl.multiple_of(odd * last, LANES), width)]
    copies = [
        pltpu.make_async_copy(edge_hbm, edge_ref, sems.at[0]),
        pltpu.make_async_copy(degrees_hbm, degrees_ref, sems.at[1]),
        pltpu.make_async_copy(basis_hbm, basis_ref, sems.at[2]),
        pltpu.make_async_copy(columns_hbm, columns_ref, sems.at[3]),
    ]
    for copy in copies:
        copy.start()
    for copy in copies[:2]:
        copy.wait()
    for i in range(width // LANES):
        columns = slice(i * LANES, (i + 1) * LANES)
        far_ref[:, columns] = scaled(degrees_ref, odd * (last // LANES) + i, edge_ref[:, columns])
    for copy in copies[2:]:
        copy.wait()


def own_kernel(count, block, edges, place_ref, columns_ref, basis_ref, degrees_ref, affinity_ref, *refs):
    near_refs, (partial_ref, gram_ref, extended) = refs[:REACH], refs[REACH:]
    pieces = block // LANES
    for b in range(REACH):
        extended[b] = jnp.zeros_like(extended[b])
        extended[count + REACH + b] = jnp.zeros_like(extended[b])
    for piece in range(count * pieces):
        b, c = divmod(piece, pieces)
        basis = basis_ref[:, piece * LANES:(piece + 1) * LANES]
        extended[REACH + b, :, c * LANES:(c + 1) * LANES] = scaled(degrees_ref, piece, basis)
    odd = place_ref[0] % 2
    for b in range(REACH):
        near_refs[b][...] = extended[REACH + (1 - odd) * (count - REACH) + b]
    first = place_ref[0] * count - REACH
    inner = []
    for b in range(count):
        total = rank_dot(extended[REACH + b], affinity_ref[b, 0], (1, 1))
        for slot in range(1, affinity_ref.shape[1]):
            total += rank_dot(extended[columns_ref[slot, b] - first], affinity_ref[b, slot], (1, 1))
        if b not in edges:
            total *= block_root(degrees_ref, b, block)
            inner.append(split(total))
        partial_ref[:, b * block:(b + 1) * block] = total
    if inner:
        gram_ref[...] = gram_halves(jnp.concatenate(inner, axis=1))
    else:
        gram_ref[...] = jnp.zeros_like(gram_ref)


def side_images(count, block, left, place_ref, columns_ref, degrees_ref, affinity_ref, partial_ref, halo):
    first = place_ref[0] * count - REACH
    pieces = block // LANES
    slots = affinity_ref.shape[1]
    images = []
    for r in range(REACH):
        row = jnp.where(left, r, count - 1 - r)
        total = partial_ref[:, pl.ds(pl.multiple_of(row * block, block), block)]
        named = [columns_ref[slot, row] - first for slot in range(slots)]
        beyond = [(index < REACH) | (index >= REACH + count) for index in named]
        picks = [(slot, named[slot], beyond[slot]) for slot in range(1, slots)]
        if REACH - r == 1:
            slot, index, outside = picks[0]
            for other, other_index, other_outside in picks[1:]:
                slot, index = jnp.where(other_outside, other, slot), jnp.where(other_outside, other_index, index)
                outside = outside | other_outside
            picks = [(slot, index, outside)]
        for slot, index, outside in picks:
            index = jnp.where(index < REACH, index, index - REACH - count)
            picked = jnp.zeros_like(halo[0])
            for b in range(REACH):
                picked = jnp.where(outside & (index == b), halo[b], picked)
            total += rank_dot(picked, affinity_ref[row, slot], (1, 1))
        root = [inverse_root(degrees_ref, row * pieces + c) for c in range(pieces)]
        images.append(split(total * jnp.concatenate(root, axis=1)))
    placed = [jnp.where(left, near, far) for near, far in zip(images, images[::-1])]
    return jnp.concatenate(images, axis=1), jnp.concatenate(placed, axis=1)


def near_kernel(count, block, place_ref, columns_ref, degrees_ref, *refs):
    near_refs, (affinity_ref, partial_ref, own_gram_ref, image_ref, gram_ref) = refs[:REACH], refs[REACH:]
    halo = [ref[...] for ref in near_refs]
    left = place_ref[0] % 2 == 1
    image, placed = side_images(count, block, left, place_ref, columns_ref, degrees_ref, affinity_ref, partial_ref, halo)
    image_ref[...] = placed
    gram_ref[...] = own_gram_ref[...] + gram_halves(image)


def far_kernel(
    count, block, late, place_ref, columns_ref, degrees_ref, rest_ref, most_ref, affinity_ref, partial_ref, near_gram_ref,
    image_ref, gram_ref
):
    is_late = (place_ref[0] == late[0]) | (place_ref[0] == late[1])
    halo = []
    for b in range(REACH):
        columns = slice(b * block, (b + 1) * block)
        halo.append(jnp.where(is_late, rest_ref[:, columns], most_ref[:, columns]))
    left = place_ref[0] % 2 == 0
    image, placed = side_images(count, block, left, place_ref, columns_ref, degrees_ref, affinity_ref, partial_ref, halo)
    image_ref[...] = placed
    halves = near_gram_ref[...] + gram_halves(image)
    rank = halves.shape[0]
    halves = halves + pltpu.roll(halves, rank, 1)
    lane = lax.broadcasted_iota(jnp.int32, gram_ref.shape, 1)
    gram_ref[...] = jnp.where(lane < rank, halves[:rank // 2], halves[rank // 2:])


def reorder_kernel(count, block, edges, place_ref, inner_ref, near_ref, far_ref, reorder_ref, placed_ref):
    odd = place_ref[0] % 2 == 1
    source = lax.broadcasted_iota(jnp.int32, (block, block), 0)
    for b in range(count):
        if b in edges:
            columns = slice(b % REACH * block, (b % REACH + 1) * block)
            nearer = odd if b < REACH else ~odd
            terms = jnp.where(nearer, near_ref[:, columns], far_ref[:, columns])
        else:
            terms = split(inner_ref[:, b * block:(b + 1) * block])
        chosen = jnp.where(source == reorder_ref[b:b + 1, :], 1.0, 0.0).astype(jnp.bfloat16)
        moved = rank_dot(terms, chosen, (1, 0))
        moved = moved.astype(jnp.bfloat16)
        rank = terms.shape[0] // 2
        placed_ref[:2 * rank, b * block:(b + 1) * block] = moved
        placed_ref[2 * rank:, b * block:(b + 1) * block] = moved[:rank]


def along_lanes(x, column):
    return jnp.broadcast_to(x[:, column:column + 1], (SUBLANES, LANES))


def along_sublanes(x, row):
    return jnp.broadcast_to(x[row:row + 1, :], (SUBLANES, LANES))


def inverse_factor(folded):
    rank = folded.shape[1] // 2
    tiles, per = rank // SUBLANES, 2
    size = per * SUBLANES
    rows = lax.broadcasted_iota(jnp.int32, (rank, 2 * rank), 0)
    columns = lax.broadcasted_iota(jnp.int32, (rank, 2 * rank), 1)
    state = jnp.concatenate([folded, pltpu.roll(folded, rank, 1)], axis=0)
    state = jnp.where(columns < rank, state, jnp.where(columns - rank == rows, 1.0, 0.0))
    state = [state[SUBLANES * t:SUBLANES * (t + 1)] for t in range(tiles)]
    sublane = lax.broadcasted_iota(jnp.int32, (SUBLANES, LANES), 0)
    for top in range(0, tiles, per):
        at = top * SUBLANES
        live = [{t: along_lanes(state[t], at + j) for t in range(top, tiles)} for j in range(size)]
        diagonal = {}
        pivot = along_sublanes(live[0][top], 0)
        for i in range(size):
            tile, s = top + i // SUBLANES, i % SUBLANES
            inverse = 1.0 / pivot
            diagonal[tile] = jnp.where(sublane == s, pivot, diagonal[tile]) if s else pivot
            ahead = {j: along_sublanes(live[j][tile], s) for j in range(i + 1, size)}
            if ahead:
                tile_next, s_next = top + (i + 1) // SUBLANES, (i + 1) % SUBLANES
                pivot = along_sublanes(live[i + 1][tile_next], s_next) - along_sublanes(
                    live[i][tile_next], s_next
                ) * (ahead[i + 1] * inverse)
            row = along_sublanes(state[tile], s)
            for t in range(tile, tiles):
                column = live[i][t] * inverse
                for j in ahead:
                    live[j][t] = live[j][t] - column * ahead[j]
                if t == tile:
                    column = jnp.where(sublane > s, column, 0.0)
                state[t] = state[t] - column * row
        for t in range(top, top + per):
            state[t] = state[t] * lax.rsqrt(diagonal[t])
    return jnp.concatenate(state, axis=0)


def targets_kernel(total_items, parts, *refs):
    placed_ref, targets_hbm, targets_ref, sems = refs[parts:]
    gram = refs[0][...]
    for part in refs[1:parts]:
        gram = gram + part[...]
    right = inverse_factor(gram) * math.sqrt(total_items)
    rank = right.shape[0]
    left = pltpu.roll(right, rank, 1)
    lane = lax.broadcasted_iota(jnp.int32, right.shape, 1)
    high = jnp.where(lane < rank, left, right).astype(jnp.bfloat16)
    low = (left - left.astype(jnp.bfloat16).astype(jnp.float32)).astype(jnp.bfloat16)
    left = jnp.concatenate([high, low[:, :rank]], axis=1)
    chunk = targets_ref.shape[1] // CHUNKS
    copies = []
    for c in range(CHUNKS):
        columns = slice(c * chunk, (c + 1) * chunk)
        targets_ref[:, columns] = rank_dot(left, placed_ref[:, columns], (1, 0))
        copies.append(pltpu.make_async_copy(targets_ref.at[:, columns], targets_hbm.at[:, columns], sems.at[c]))
        copies[-1].start()
    for copy in copies:
        copy.wait()


def gram_parts(gram, mesh_size):
    if mesh_size & (mesh_size - 1):
        return [lax.psum(gram, AXES)]
    bits = [1 << k for k in range(1, mesh_size.bit_length() - 1)]
    rounds = [[1]] + [[bit | 1] for bit in bits[2:]]
    if bits:
        rounds.append([bit | 1 for bit in bits[1::-1]] + [sum(bits[:2]) | 1] * (len(bits) > 1))
    parts = [gram]
    for masks in rounds:
        gram = sum(parts[1:], parts[0])
        parts = [gram] + [lax.ppermute(gram, AXES, [(i, i ^ mask) for i in range(mesh_size)]) for mask in masks]
    return parts


def cycle(*devices):
    return list(zip(devices, devices[1:] + devices[:1]))


def crossing_pairs(mesh_size):
    n = mesh_size
    if n % 2 or n < 8:
        pairs = [pair for i in range(1, n - 1, 2) for pair in cycle(i, i + 1)]
        return [pairs, pairs]
    most = [pair for i in range(3, n - 4, 2) for pair in cycle(i, i + 1)]
    most += cycle(2, 1, 0) + cycle(n - 3, n - 2, n - 1)
    rest = [pair for i in range(4, n - 4, 2) for pair in cycle(i, i + 1)]
    rest += cycle(1, 2, 3, 0) + cycle(n - 2, n - 3, n - 4, n - 1)
    return [rest, most]


def body(mesh_size, affinity, old_basis, degrees, column_blocks, reorder):
    count, slots, block, _ = affinity.shape
    items, rank = old_basis.shape
    width = REACH * block
    assert count % REACH == 0 and count >= 2 * REACH
    edges = [b for b in range(count) if b < REACH or b >= count - REACH]
    affinity = in_vmem(affinity)
    basis = old_basis.T
    degree_rows = degrees.reshape(items // LANES, LANES)
    columns = column_blocks.T
    place = lax.axis_index(AXES).astype(jnp.int32).reshape(1)
    folded = pltpu.VMEM((rank // 2, 2 * rank), jnp.float32)

    far, columns, basis, degree_rows = pl.pallas_call(
        functools.partial(edges_kernel, width),
        out_shape=(
            pltpu.VMEM((rank, width), jnp.bfloat16),
            pltpu.SMEM(columns.shape, jnp.int32),
            pltpu.VMEM(basis.shape, jnp.bfloat16),
            pltpu.VMEM(degree_rows.shape, jnp.int32),
        ),
        in_specs=[SMEM, HBM, HBM, HBM],
        out_specs=(VMEM, SMEM, VMEM, VMEM),
        scratch_shapes=[pltpu.VMEM((rank, width), jnp.bfloat16), pltpu.SemaphoreType.DMA((4,))],
        compiler_params=PARAMS,
        cost_estimate=pl.CostEstimate(flops=1000 * affinity.size, bytes_accessed=40 * affinity.size, transcendentals=0),
        name="edges",
    )(place, *map(in_hbm, (columns, basis, degree_rows)))
    distant = [lax.ppermute(far, AXES, pairs) for pairs in crossing_pairs(mesh_size)]

    *near, partial, inner = pl.pallas_call(
        functools.partial(own_kernel, count, block, edges),
        out_shape=(
            *[pltpu.VMEM((rank, block), jnp.bfloat16)] * REACH,
            pltpu.VMEM((rank, items), jnp.float32),
            pltpu.VMEM((rank, 2 * rank), jnp.float32),
        ),
        in_specs=[SMEM, SMEM] + [VMEM] * 3,
        out_specs=(VMEM,) * (2 + REACH),
        scratch_shapes=[pltpu.VMEM((count + 2 * REACH, rank, block), jnp.bfloat16)],
        compiler_params=PARAMS,
        cost_estimate=pl.CostEstimate(
            flops=2 * count * slots * block * block * rank, bytes_accessed=0, transcendentals=0
        ),
        name="own",
    )(place, columns, *map(in_vmem, (basis, degree_rows)), affinity)
    near = [lax.ppermute(x, AXES, [(i, i ^ 1) for i in range(mesh_size) if i ^ 1 < mesh_size]) for x in near]

    side = dict(
        out_specs=(VMEM, VMEM),
        compiler_params=PARAMS,
        cost_estimate=pl.CostEstimate(flops=1, bytes_accessed=1, transcendentals=0),
    )
    side_image = pltpu.VMEM((2 * rank, width), jnp.bfloat16)
    near_image, gram = pl.pallas_call(
        functools.partial(near_kernel, count, block),
        out_shape=(side_image, pltpu.VMEM((rank, 2 * rank), jnp.float32)),
        in_specs=[SMEM, SMEM] + [VMEM] * (4 + REACH),
        name="near",
        **side,
    )(place, columns, *map(in_vmem, (degree_rows, *near)), affinity, *map(in_vmem, (partial, inner)))
    far_image, gram = pl.pallas_call(
        functools.partial(far_kernel, count, block, (2, mesh_size - 3)),
        out_shape=(side_image, folded),
        in_specs=[SMEM, SMEM] + [VMEM] * 6,
        name="far",
        **side,
    )(place, columns, *map(in_vmem, (degree_rows, *distant)), affinity, *map(in_vmem, (partial, gram)))

    placed = pl.pallas_call(
        functools.partial(reorder_kernel, count, block, edges),
        out_shape=pltpu.VMEM((3 * rank, items), jnp.bfloat16),
        in_specs=[SMEM] + [VMEM] * 4,
        out_specs=VMEM,
        compiler_params=PARAMS,
        cost_estimate=pl.CostEstimate(flops=4 * rank * items * block, bytes_accessed=0, transcendentals=0),
        name="reorder",
    )(place, *map(in_vmem, (partial, near_image, far_image, reorder)))

    parts = gram_parts(gram, mesh_size)
    targets = pl.pallas_call(
        functools.partial(targets_kernel, items * mesh_size, len(parts)),
        out_shape=jax.ShapeDtypeStruct((rank, items), jnp.float32),
        in_specs=[VMEM] * (len(parts) + 1),
        out_specs=HBM,
        scratch_shapes=[pltpu.VMEM((rank, items), jnp.float32), pltpu.SemaphoreType.DMA((CHUNKS,))],
        compiler_params=PARAMS,
        name="targets",
    )(*map(in_vmem, parts), in_vmem(placed))
    return targets.T


def solution(mesh):
    placed = (
        P(AXES, None, None, None),
        P(AXES, None),
        P(AXES),
        P(AXES, None),
        P(AXES, None),
    )
    mesh_size = mesh.shape["rows"] * mesh.shape["sub"]
    return jax.shard_map(
        functools.partial(body, mesh_size), mesh=mesh, in_specs=placed, out_specs=P(AXES, None), check_vma=False
    )
```
